32 devices in a mesh: rows: 8 (over z, y), mem: 4 (over x, core).
Axes of the slice: x: 2, y: 2, z: 4, core: 2. Of those that a mesh axis runs over, the one named last changes fastest.
Arguments:
- state: float32 [2048, 5120], P('rows', 'mem')
- member_level: int32 [5120], P('mem'), may hold values from 0 to 3, as said below
- level_weight: float32 [4], replicated, may hold values from 0.3 to 3
- obs_row: int32 [128], replicated, may hold values from 0 to 2047
- state_coords: int32 [2, 2048], replicated, may hold values from 0 to 63, as said below
- weights: float32 [128, 5120], P('rows', 'mem'), may hold values from -6 to 6
Outputs:
- increment: float32 [2048, 5120], P('rows', 'mem')
The draws below stay inside these ranges and needn't reach their ends.
Inputs may be any that keep to these rules, and one draw needn't show every extreme that they name: `member_level`: every one of the 4 levels holds at least 2 members. `state_coords`: the first coordinate of row i lies within 2 of i // 64.
All inputs are finite; a program needn't handle non-finite values.
Results may differ from the reference program's by a relative error of at most 0.000073.
Values sent between devices are 32-bit elements; how exact they have to be, the bound alone decides.
No kernel may reach another device: no remote copies, remote signals or barrier semaphores. Data moves between devices by JAX's collectives and lax.ppermute only.
A program may use at most 64 MiB of HBM per device.

```python
import math
import jax
import jax.numpy as jnp
from jax import lax

LEVELS = 4
NS = 2048
M = 5120
NO = 128
GX = 32
GY = 64
RADIUS = 32


def member_levels(key):
    inner = jax.random.fold_in(key, 11)
    first_key, second_key = jax.random.split(inner)
    base = jax.random.randint(first_key, (M,), 0, LEVELS)
    order = jax.random.permutation(second_key, M)
    forced = jnp.arange(2 * LEVELS, dtype=jnp.int32) % LEVELS
    return base.at[order[:2 * LEVELS]].set(forced)


def draw_member_level(key, part):
    return member_levels(key).astype(jnp.int32)


def draw_state(key, part):
    levels = member_levels(key)
    inner = jax.random.fold_in(key, 23)
    keys = jax.random.split(inner, 4)
    row_mean = 3.0 * jax.random.normal(keys[0], (NS, 1), jnp.float32)
    bias = jax.random.normal(keys[1], (NS, LEVELS), jnp.float32)
    spread = jnp.exp(jax.random.uniform(keys[2], (NS, 1), jnp.float32, jnp.log(0.3), jnp.log(3.0)))
    noise = jax.random.normal(keys[3], (NS, M), jnp.float32)
    return (row_mean + jnp.take(bias, levels, axis=1) + spread * noise).astype(jnp.float32)


def draw_state_coords(key, part):
    inner = jax.random.fold_in(key, 31)
    first_key, second_key = jax.random.split(inner)
    jitter = jax.random.randint(first_key, (NS,), -2, 3)
    first = jnp.clip(jnp.arange(NS, dtype=jnp.int32) // GY + jitter, 0, GX - 1)
    second = jax.random.randint(second_key, (NS,), 0, GY)
    return jnp.stack([first, second]).astype(jnp.int32)


def with_ends(drawn, stream_key, low, largest):
    spot = [jax.random.randint(jax.random.fold_in(stream_key, axis), (), 0, length) for axis, length in enumerate(drawn.shape)]
    main_axis = drawn.shape.index(max(drawn.shape))
    neighbour = spot[:main_axis] + [(spot[main_axis] + 1) % drawn.shape[main_axis]] + spot[main_axis + 1:]
    return drawn.at[tuple(spot)].set(low).at[tuple(neighbour)].set(largest)


def block_scale(key, shape, shards, low, high):
    loudness = 1.0
    for dim, parts in shards:
        draws = jax.random.uniform(jax.random.fold_in(jax.random.fold_in(key, 6), dim), (parts,), jnp.float32, low / len(shards), high / len(shards))
        loudness = loudness * jnp.repeat(jnp.exp(draws), shape[dim] // parts).reshape((-1,) + (1,) * (len(shape) - 1 - dim))
    return loudness


def scatter_about(own_key, dims, width, most, pieces=(), kind=jnp.bfloat16):
    gain = block_scale(own_key, dims, pieces, -0.22, 0.18) if pieces else 1.0
    array = jax.random.normal(own_key, dims, jnp.float32) * width * gain
    return jnp.minimum(jnp.maximum(array, -most), most).astype(kind)


def setup_inputs(seed: int = 0) -> dict:
    key_list = jax.random.split(jax.random.key(seed), 7)
    state = draw_state(jax.random.fold_in(key_list[6], 71), 0)
    member_level = draw_member_level(jax.random.fold_in(key_list[6], 71), 0)
    level_weight = jnp.clip(jnp.exp(jax.random.uniform(key_list[2], (LEVELS,), jnp.float32, math.log(0.3), math.log(3.0))), 0.3, 3.0)
    obs_row = with_ends(jax.random.randint(key_list[3], (NO,), 0, NS), jax.random.fold_in(key_list[3], 1), 0, NS - 1).astype(jnp.int32)
    state_coords = draw_state_coords(jax.random.fold_in(key_list[6], 71), 0)
    weights = scatter_about(key_list[5], (NO, M), 1.0, 6.0, ((0, 8), (1, 4)), jnp.float32)
    return dict(state=state, member_level=member_level, level_weight=level_weight, obs_row=obs_row, state_coords=state_coords, weights=weights)


def reference(state, member_level, level_weight, obs_row, state_coords, weights):
    highest = lax.Precision.HIGHEST
    onehot = (member_level[:, None] == jnp.arange(LEVELS, dtype=jnp.int32)[None, :]).astype(jnp.float32)
    counts = jnp.sum(onehot, axis=0)
    sums = jnp.dot(state, onehot, precision=highest, preferred_element_type=jnp.float32)
    means = sums / counts[None, :]
    anomaly = state - jnp.take(means, member_level, axis=1)
    level_scale = level_weight / (counts - 1.0)
    scaled = anomaly * jnp.take(level_scale, member_level)[None, :]
    observed = jnp.take(anomaly, obs_row, axis=0)
    cross = jnp.dot(scaled, observed.T, precision=highest, preferred_element_type=jnp.float32)
    observed_xy = jnp.take(state_coords, obs_row, axis=1)
    offset_x = state_coords[0][:, None] - observed_xy[0][None, :]
    offset_y = state_coords[1][:, None] - observed_xy[1][None, :]
    distance = offset_x * offset_x + offset_y * offset_y
    reach = jnp.maximum(0.0, 1.0 - distance.astype(jnp.float32) / float(RADIUS * RADIUS))
    tapered = cross * (reach * reach)
    return jnp.dot(tapered, weights, precision=highest, preferred_element_type=jnp.float32)
```

```python
import functools
import math

import jax
import jax.numpy as jnp
from jax import lax
from jax.experimental import pallas as pl
from jax.experimental.pallas import tpu as pltpu
from jax.sharding import PartitionSpec as P

LEVELS = 4
XCOL_DEV = 4
SUB = 8
VMEM_LIMIT = 48 * 1024 * 1024
F32 = jnp.float32
BF16 = jnp.bfloat16
LANES_BOTH = (((1,), (1,)), ((), ()))
ROWS_BOTH = (((0,), (0,)), ((), ()))
PLAIN = (((1,), (0,)), ((), ()))


def dot(a, b, dims):
    return lax.dot_general(a, b, dims, preferred_element_type=F32)


def split(x, parts):
    pieces = []
    for _ in range(parts - 1):
        piece = x.astype(BF16)
        pieces.append(piece)
        x = x - piece.astype(F32)
    pieces.append(x.astype(BF16))
    return pieces


def level_onehot(level_row):
    levels = lax.broadcasted_iota(jnp.int32, (SUB, level_row.shape[1]), 0)
    return (level_row == levels).astype(F32)


def by_level(level_row, columns):
    picked = jnp.where(level_row == 1, columns[1], columns[0])
    for level in range(2, LEVELS):
        picked = jnp.where(level_row == level, columns[level], picked)
    return picked


def pick_kernel(obs_ref, skip_ref, state_ref, out_ref):
    rows = state_ref.shape[0]
    slots = out_ref.shape[0]
    row_first = lax.axis_index("rows") * rows
    skip = skip_ref[0]

    def visit(j, rank):
        row = obs_ref[j] - row_first
        mine = (row >= 0) & (row < rows)
        slot = rank - skip

        @pl.when(mine & (slot >= 0) & (slot < slots))
        def _():
            out_ref[pl.ds(slot, 1), :] = state_ref[pl.ds(row, 1), :]

        return rank + mine.astype(jnp.int32)

    total = lax.fori_loop(0, obs_ref.shape[0], visit, 0, unroll=8)

    def clear(slot, carry):
        out_ref[pl.ds(slot, 1), :] = jnp.zeros((1, out_ref.shape[1]), F32)
        return carry

    lax.fori_loop(jnp.clip(total - skip, 0, slots), slots, clear, 0)


def pick(obs_row, skip, state, slots):
    smem = pl.BlockSpec(memory_space=pltpu.SMEM)
    vmem = pl.BlockSpec(memory_space=pltpu.VMEM)
    return pl.pallas_call(
        pick_kernel,
        out_shape=jax.ShapeDtypeStruct((slots, state.shape[1]), F32),
        in_specs=[smem, smem, vmem],
        out_specs=vmem,
        compiler_params=pltpu.CompilerParams(vmem_limit_bytes=VMEM_LIMIT),
        name="pick",
    )(obs_row, skip, state)


def center_kernel(level_ref, state_ref, sums_ref, high_ref, low_ref):
    level_row = level_ref[...]
    onehot = level_onehot(level_row)
    counts = jnp.sum(onehot, axis=1, keepdims=True)
    state = state_ref[...]
    hot = onehot.astype(BF16)
    sums = sum(dot(hot, piece, LANES_BOTH) for piece in split(state, 3))
    sums_ref[0:LEVELS, :] = sums[0:LEVELS, :]
    sums_ref[LEVELS:SUB, :] = jnp.broadcast_to(counts[0:LEVELS, :], (LEVELS, sums.shape[1]))
    means = jnp.transpose(sums / jnp.maximum(counts, 1.0))
    columns = [means[:, level : level + 1] for level in range(LEVELS)]
    high, low = split(state - by_level(level_row, columns), 2)
    high_ref[...] = high
    low_ref[...] = low


def center(level_row, state):
    rows, members = state.shape
    vmem = pl.BlockSpec(memory_space=pltpu.VMEM)
    return pl.pallas_call(
        center_kernel,
        out_shape=(
            jax.ShapeDtypeStruct((SUB, rows), F32),
            jax.ShapeDtypeStruct((rows, members), BF16),
            jax.ShapeDtypeStruct((rows, members), BF16),
        ),
        in_specs=[vmem, vmem],
        out_specs=(vmem, vmem, vmem),
        compiler_params=pltpu.CompilerParams(vmem_limit_bytes=VMEM_LIMIT),
        name="center",
    )(level_row, state)


def cross_kernel(number, slots, weight_ref, skip_ref, level_ref, counts_ref, place_ref, high_ref, low_ref, before_ref, *refs):
    blocks, out_ref = refs[: len(number)], refs[len(number)]
    o_high, o_low, p_ref, m_ref = refs[len(number) + 1 :]
    rows = high_ref.shape[0]
    me = lax.axis_index("rows")
    skip = skip_ref[0]
    level_row = level_ref[...]
    onehot = level_onehot(level_row)
    counts = jnp.maximum(jnp.sum(onehot, axis=1, keepdims=True), 1.0)
    total = jnp.sum(counts_ref[...], axis=0)
    scales = [weight_ref[level] / (total[level, 0] - 1.0) for level in range(LEVELS)]
    member_scale = by_level(level_row, scales)
    owner, rank = place_ref[0:1, :], place_ref[1:2, :]
    padded = o_high.shape[0] // len(number)
    m_ref[...] = jnp.zeros_like(m_ref)
    for n, block_ref in enumerate(blocks):
        at = n * padded
        block = block_ref[...]
        columns = []
        for level in range(LEVELS):
            member = jnp.where(level_row == level, block, 0.0)
            columns.append(jnp.sum(member, axis=1, keepdims=True) / counts[level : level + 1, :])
            m_ref[at : at + slots, level : level + 1] = columns[level]
        high, low = split((block - by_level(level_row, columns)) * member_scale, 2)
        o_high[at : at + slots, :] = high
        o_low[at : at + slots, :] = low
        slot = lax.broadcasted_iota(jnp.int32, (slots, owner.shape[1]), 0)
        hit = (owner == (me ^ number[n])) & (rank - skip == slot)
        p_ref[at : at + slots, :] = hit.astype(BF16)
    by_slot = dot(high_ref[...], o_high[...], LANES_BOTH)
    by_slot += dot(high_ref[...], o_low[...], LANES_BOTH)
    by_slot += dot(low_ref[...], o_high[...], LANES_BOTH)
    place = p_ref[...]
    cross = sum(dot(piece, place, PLAIN) for piece in split(by_slot, 3))
    out_ref[0:rows, :] = before_ref[0:rows, :] + cross
    means = sum(dot(piece, place, ROWS_BOTH) for piece in split(m_ref[...], 3))
    out_ref[rows : rows + SUB, :] = before_ref[rows : rows + SUB, :] + means


def cross_part(level_weight, skip, level_row, counts, place, high, low, before, blocks, number):
    rows, members = high.shape
    slots = blocks[0].shape[0]
    smem = pl.BlockSpec(memory_space=pltpu.SMEM)
    vmem = pl.BlockSpec(memory_space=pltpu.VMEM)
    held = len(number) * slots
    return pl.pallas_call(
        functools.partial(cross_kernel, number, slots),
        out_shape=jax.ShapeDtypeStruct(before.shape, F32),
        in_specs=[smem, smem] + [vmem] * (6 + len(number)),
        out_specs=vmem,
        scratch_shapes=[
            pltpu.VMEM((held, members), BF16),
            pltpu.VMEM((held, members), BF16),
            pltpu.VMEM((held, before.shape[1]), BF16),
            pltpu.VMEM((held, SUB), F32),
        ],
        compiler_params=pltpu.CompilerParams(vmem_limit_bytes=VMEM_LIMIT),
        name="cross_part",
    )(level_weight, skip, level_row, counts, place, high, low, before, *blocks)


def final_kernel(number, weight_ref, parts_ref, sums_ref, taper_ref, *refs):
    blocks, out_ref = refs[: len(number)], refs[len(number)]
    t_high, t_low, w_high, w_low = refs[len(number) + 1 :]
    step = pl.program_id(0)
    rows = taper_ref.shape[0]
    me = lax.axis_index("rows")
    mem = parts_ref.shape[0]

    @pl.when(step == 0)
    def _():
        cross = sum(parts_ref[d, 0:rows, :] for d in range(mem))
        counts = [sums_ref[d, LEVELS:SUB, :] for d in range(mem)]
        sums = [sums_ref[d, 0:LEVELS, :] for d in range(mem)]
        total = sum(counts)
        mean = sum(sums) / total
        level = lax.broadcasted_iota(jnp.int32, (LEVELS, 1), 0)
        scale = by_level(level, [weight_ref[k] for k in range(LEVELS)]) / (total - 1.0)
        me_mem = lax.axis_index("mem")
        seen = [parts_ref[me_mem ^ d, rows : rows + LEVELS, :] for d in range(mem)]
        seen_counts = [c[:, 0:1] for c in counts]
        seen_mean = sum(c * s for c, s in zip(seen_counts, seen)) / total[:, 0:1]
        left, right = [], []
        for d in range(mem):
            left.append(scale * (sums[d] - counts[d] * mean))
            right.append(jnp.where(seen_counts[d] > 0.0, seen[d] - seen_mean, 0.0))
        left = split(jnp.concatenate(left, axis=0), 2)
        right = split(jnp.concatenate(right, axis=0), 2)
        cross += dot(left[0], right[0], ROWS_BOTH)
        cross += dot(left[0], right[1], ROWS_BOTH)
        cross += dot(left[1], right[0], ROWS_BOTH)
        high, low = split(cross * taper_ref[...], 2)
        t_high[...] = high
        t_low[...] = low

    for n, block_ref in enumerate(blocks):
        length = block_ref.shape[0]
        at = pl.multiple_of((me ^ number[n]) * length, length)
        high, low = split(block_ref[...], 2)
        w_high[pl.ds(at, length), :] = high
        w_low[pl.ds(at, length), :] = low
    out = dot(t_high[...], w_high[...], PLAIN)
    out += dot(t_high[...], w_low[...], PLAIN)
    out += dot(t_low[...], w_high[...], PLAIN)
    out_ref[...] = out


def final(level_weight, parts, sums, taper, blocks, number):
    rows, observed = taper.shape
    length, members = blocks[0].shape
    width = math.gcd(members, 256)
    smem = pl.BlockSpec(memory_space=pltpu.SMEM)
    vmem = pl.BlockSpec(memory_space=pltpu.VMEM)
    return pl.pallas_call(
        functools.partial(final_kernel, number),
        out_shape=jax.ShapeDtypeStruct((rows, members), F32),
        grid=(members // width,),
        in_specs=[smem, vmem, vmem, vmem] + [pl.BlockSpec((length, width), lambda i: (0, i))] * len(number),
        out_specs=pl.BlockSpec((rows, width), lambda i: (0, i)),
        scratch_shapes=[
            pltpu.VMEM((rows, observed), BF16),
            pltpu.VMEM((rows, observed), BF16),
            pltpu.VMEM((observed, width), BF16),
            pltpu.VMEM((observed, width), BF16),
        ],
        compiler_params=pltpu.CompilerParams(vmem_limit_bytes=VMEM_LIMIT),
        name="final",
    )(level_weight, parts, sums, taper, *blocks)


def across(x, axis, bits):
    count = lax.axis_size(axis)
    return lax.ppermute(x, axis, [(i, i ^ bits) for i in range(count)])


def line_order(count):
    line = [2 * s for s in range(1, count // 2)]
    return [0] + sorted(line, key=lambda b: (b != 4, b))


def gather_line(x, order):
    return [x] + [across(x, "rows", b) for b in order[1:]]


def taper_rows(state_coords, obs_row, row_first, row_total, radius):
    state_xy = lax.dynamic_slice_in_dim(state_coords, row_first, row_total, 1)
    observed_xy = jnp.take(state_coords, obs_row, axis=1)
    offset_x = state_xy[0][:, None] - observed_xy[0][None, :]
    offset_y = state_xy[1][:, None] - observed_xy[1][None, :]
    distance = offset_x * offset_x + offset_y * offset_y
    reach = jnp.maximum(0.0, 1.0 - distance.astype(F32) / float(radius * radius))
    return reach * reach


def on_device(state, member_level, level_weight, obs_row, state_coords, weights):
    groups = lax.axis_size("rows")
    radius = XCOL_DEV * groups
    row_count = state.shape[0]
    observed = obs_row.shape[0]
    row_first = lax.axis_index("rows") * row_count
    order = line_order(groups)
    pair = [b ^ 1 for b in order]
    slots = min(observed, 16 * (-(-2 * observed // groups) // 16))

    none = jnp.zeros((1,), jnp.int32)
    level_row = member_level[None, :]
    own = pick(obs_row, none, state, slots)
    line = gather_line(own, order)
    other = [across(x, "rows", 1) for x in line]

    sums, high, low = center(level_row, state)
    all_sums = jnp.stack([sums] + [across(sums, "mem", b) for b in range(1, lax.axis_size("mem"))])
    counts = all_sums[:, LEVELS:, 0:128]

    owner = obs_row // row_count
    same = owner[:, None] == owner[None, :]
    earlier = lax.broadcasted_iota(jnp.int32, same.shape, 1) < lax.broadcasted_iota(jnp.int32, same.shape, 0)
    rank = jnp.sum((same & earlier).astype(jnp.int32), axis=1)
    place = jnp.stack([owner, rank])
    rounds = jnp.max(rank) // slots + 1

    cross = functools.partial(cross_part, level_weight)
    empty = jnp.zeros((row_count + SUB, observed), F32)

    def more(carry):
        return carry[0] < rounds

    def another(carry):
        turn, part = carry
        skip = (turn * slots)[None]
        block = pick(obs_row, skip, state, slots)
        near = gather_line(block, order)
        far = [across(x, "rows", 1) for x in near]
        part = cross(skip, level_row, counts, place, high, low, part, near + far, order + pair)
        return turn + 1, part

    _, part = lax.while_loop(more, another, (jnp.int32(1), empty))
    part = cross(none, level_row, counts, place, high, low, part, line, order)
    part = cross(none, level_row, counts, place, high, low, part, other, pair)

    weights_line = gather_line(weights, order)
    weights_other = [across(x, "rows", 1) for x in weights_line]
    taper = taper_rows(state_coords, obs_row, row_first, row_count, radius)

    parts = lax.all_gather(part, "mem", axis=0)
    return final(level_weight, parts, all_sums, taper, weights_line + weights_other, order + pair)


def solution(mesh):
    in_specs = (P("rows", "mem"), P("mem"), P(), P(), P(), P("rows", "mem"))
    out_specs = P("rows", "mem")
    return jax.shard_map(
        on_device, mesh=mesh, in_specs=in_specs, out_specs=out_specs, check_vma=False
    )
```

```python
import functools
import math

import jax
import jax.numpy as jnp
from jax import lax
from jax.experimental import pallas as pl
from jax.experimental.pallas import tpu as pltpu
from jax.sharding import PartitionSpec as P

LEVELS = 4
XCOL_DEV = 4
SUB = 8
VMEM_LIMIT = 48 * 1024 * 1024
COST = pl.CostEstimate(flops=1, bytes_accessed=1, transcendentals=0)
F32 = jnp.float32
BF16 = jnp.bfloat16
LANES_BOTH = (((1,), (1,)), ((), ()))
ROWS_BOTH = (((0,), (0,)), ((), ()))
PLAIN = (((1,), (0,)), ((), ()))


def dot(a, b, dims):
    return lax.dot_general(a, b, dims, preferred_element_type=F32)


def split(x, parts):
    pieces = []
    for _ in range(parts - 1):
        piece = x.astype(BF16)
        pieces.append(piece)
        x = x - piece.astype(F32)
    pieces.append(x.astype(BF16))
    return pieces


def level_onehot(level_row):
    levels = lax.broadcasted_iota(jnp.int32, (SUB, level_row.shape[1]), 0)
    return (level_row == levels).astype(F32)


def by_level(level_row, columns):
    picked = jnp.where(level_row == 1, columns[1], columns[0])
    for level in range(2, LEVELS):
        picked = jnp.where(level_row == level, columns[level], picked)
    return picked


def pick_kernel(obs_ref, skip_ref, state_ref, out_ref, list_ref):
    rows = state_ref.shape[0]
    slots = out_ref.shape[0]
    row_first = lax.axis_index("rows") * rows
    skip = skip_ref[0]

    def visit(j, rank):
        row = obs_ref[j] - row_first
        list_ref[rank] = row
        return rank + ((row >= 0) & (row < rows)).astype(jnp.int32)

    total = lax.fori_loop(0, obs_ref.shape[0], visit, 0, unroll=8)
    held = jnp.clip(total - skip, 0, slots)

    def bring(slot, carry):
        out_ref[pl.ds(slot, 1), :] = state_ref[pl.ds(list_ref[skip + slot], 1), :]
        return carry

    def clear(slot, carry):
        out_ref[pl.ds(slot, 1), :] = jnp.zeros((1, out_ref.shape[1]), F32)
        return carry

    lax.fori_loop(0, held, bring, 0)
    lax.fori_loop(held, slots, clear, 0)


def pick(obs_row, skip, state, slots):
    smem = pl.BlockSpec(memory_space=pltpu.SMEM)
    vmem = pl.BlockSpec(memory_space=pltpu.VMEM)
    return pl.pallas_call(
        pick_kernel,
        out_shape=jax.ShapeDtypeStruct((slots, state.shape[1]), F32),
        in_specs=[smem, smem, vmem],
        out_specs=vmem,
        scratch_shapes=[pltpu.SMEM((obs_row.shape[0] + 1,), jnp.int32)],
        compiler_params=pltpu.CompilerParams(vmem_limit_bytes=VMEM_LIMIT),
        cost_estimate=COST,
        name="pick",
    )(obs_row, skip, state)


def center_kernel(level_ref, state_ref, sums_ref, high_ref, low_ref):
    level_row = level_ref[...]
    onehot = level_onehot(level_row)
    counts = jnp.sum(onehot, axis=1, keepdims=True)
    state = state_ref[...]
    hot = onehot.astype(BF16)
    sums = sum(dot(hot, piece, LANES_BOTH) for piece in split(state, 3))
    sums_ref[0:LEVELS, :] = sums[0:LEVELS, :]
    sums_ref[LEVELS:SUB, :] = jnp.broadcast_to(counts[0:LEVELS, :], (LEVELS, sums.shape[1]))
    means = jnp.transpose(sums / jnp.maximum(counts, 1.0))
    columns = [means[:, level : level + 1] for level in range(LEVELS)]
    high, low = split(state - by_level(level_row, columns), 2)
    high_ref[...] = high
    low_ref[...] = low


def center(level_row, state):
    rows, members = state.shape
    tall = math.gcd(rows, 128)
    return pl.pallas_call(
        center_kernel,
        out_shape=(
            jax.ShapeDtypeStruct((SUB, rows), F32),
            jax.ShapeDtypeStruct((rows, members), BF16),
            jax.ShapeDtypeStruct((rows, members), BF16),
        ),
        grid=(rows // tall,),
        in_specs=[
            pl.BlockSpec((1, members), lambda i: (0, 0)),
            pl.BlockSpec((tall, members), lambda i: (i, 0)),
        ],
        out_specs=(
            pl.BlockSpec((SUB, tall), lambda i: (0, i)),
            pl.BlockSpec((tall, members), lambda i: (i, 0)),
            pl.BlockSpec((tall, members), lambda i: (i, 0)),
        ),
        compiler_params=pltpu.CompilerParams(vmem_limit_bytes=VMEM_LIMIT),
        cost_estimate=COST,
        name="center",
    )(level_row, state)


def place_kernel(slots, rows, obs_ref, near_ref, far_ref, place_ref, rounds_ref, pair_ref):
    observed = obs_ref.shape[1]
    length = near_ref.shape[0]
    pair_ref[0:length, :] = near_ref[...]
    pair_ref[length : 2 * length, :] = far_ref[...]
    owner = lax.div(obs_ref[...], jnp.int32(rows))
    owner_row = owner.astype(F32)
    owner_down = jnp.transpose(jnp.broadcast_to(owner_row, (SUB, observed)))[:, 0:1]
    j_down = lax.broadcasted_iota(jnp.int32, (observed, observed), 0)
    j_row = lax.broadcasted_iota(jnp.int32, (observed, observed), 1)
    earlier = (owner_down == owner_row) & (j_down < j_row)
    rank = jnp.sum(earlier.astype(F32), axis=0, keepdims=True).astype(jnp.int32)
    place_ref[0:1, :] = owner
    place_ref[1:2, :] = rank
    place_ref[2:SUB, :] = jnp.zeros((SUB - 2, observed), jnp.int32)
    rounds_ref[0] = lax.div(jnp.max(rank), jnp.int32(slots)) + 1


def places(obs_row, near, far, rows, slots):
    observed = obs_row.shape[0]
    length, members = near.shape
    vmem = pl.BlockSpec(memory_space=pltpu.VMEM)
    smem = pl.BlockSpec(memory_space=pltpu.SMEM)
    return pl.pallas_call(
        functools.partial(place_kernel, slots, rows),
        out_shape=(
            jax.ShapeDtypeStruct((SUB, observed), jnp.int32),
            jax.ShapeDtypeStruct((1,), jnp.int32),
            jax.ShapeDtypeStruct((2 * length, members), F32),
        ),
        in_specs=[vmem] * 3,
        out_specs=(vmem, smem, vmem),
        compiler_params=pltpu.CompilerParams(vmem_limit_bytes=VMEM_LIMIT),
        name="places",
    )(obs_row[None, :], near, far)


def taper_kernel(radius, obs_ref, coords_ref, taper_ref):
    rows, observed = taper_ref.shape
    total = coords_ref.shape[1]
    chunk = math.gcd(total, 256)
    obs = obs_ref[...]

    def look(n, seen):
        at = pl.multiple_of(n * chunk, chunk)
        row = lax.broadcasted_iota(jnp.int32, (chunk, observed), 0) + at
        coords = coords_ref[:, pl.ds(at, chunk)].astype(F32).astype(BF16)
        return seen + dot(coords, (row == obs).astype(BF16), PLAIN)

    seen = lax.fori_loop(0, total // chunk, look, jnp.zeros((2, observed), F32), unroll=min(8, total // chunk))
    first = pl.multiple_of(lax.axis_index("rows") * rows, rows)
    own = coords_ref[:, pl.ds(first, rows)].astype(F32)
    own_x = jnp.transpose(jnp.broadcast_to(own[0:1, :], (SUB, rows)))[:, 0:1]
    own_y = jnp.transpose(jnp.broadcast_to(own[1:2, :], (SUB, rows)))[:, 0:1]
    offset_x = own_x - seen[0:1, :]
    offset_y = own_y - seen[1:2, :]
    distance = offset_x * offset_x + offset_y * offset_y
    reach = jnp.maximum(0.0, 1.0 - distance / float(radius * radius))
    taper_ref[...] = reach * reach


def tapers(obs_row, state_coords, rows, radius):
    vmem = pl.BlockSpec(memory_space=pltpu.VMEM)
    return pl.pallas_call(
        functools.partial(taper_kernel, radius),
        out_shape=jax.ShapeDtypeStruct((rows, obs_row.shape[0]), F32),
        in_specs=[vmem, vmem],
        out_specs=vmem,
        compiler_params=pltpu.CompilerParams(vmem_limit_bytes=VMEM_LIMIT),
        name="tapers",
    )(obs_row[None, :], state_coords)


def cross_kernel(number, slots, weight_ref, skip_ref, level_ref, place_ref, high_ref, low_ref, before_ref, *refs):
    blocks, (sums_ref, out_ref, o_high, o_low, p_ref, m_ref) = refs[: len(number)], refs[len(number) :]
    rows = high_ref.shape[0]
    me = lax.axis_index("rows")
    skip = skip_ref[0]
    level_row = level_ref[...]
    onehot = level_onehot(level_row)
    counts = jnp.maximum(jnp.sum(onehot, axis=1, keepdims=True), 1.0)
    total = sum(
        sums_ref[at + LEVELS : at + SUB, 0:128] for at in range(0, sums_ref.shape[0], SUB)
    )
    scales = [weight_ref[level] / (total[level, 0] - 1.0) for level in range(LEVELS)]
    member_scale = by_level(level_row, scales)
    owner, rank = place_ref[0:1, :], place_ref[1:2, :]
    padded = o_high.shape[0] // len(number)
    m_ref[...] = jnp.zeros_like(m_ref)
    for n, block_ref in enumerate(blocks):
        at = n * padded
        block = block_ref[...]
        columns = []
        for level in range(LEVELS):
            member = jnp.where(level_row == level, block, 0.0)
            columns.append(jnp.sum(member, axis=1, keepdims=True) / counts[level : level + 1, :])
            m_ref[at : at + slots, level : level + 1] = columns[level]
        high, low = split((block - by_level(level_row, columns)) * member_scale, 2)
        o_high[at : at + slots, :] = high
        o_low[at : at + slots, :] = low
        slot = lax.broadcasted_iota(jnp.int32, (slots, owner.shape[1]), 0)
        hit = (owner == (me ^ number[n])) & (rank - skip == slot)
        p_ref[at : at + slots, :] = hit.astype(BF16)
    by_slot = dot(high_ref[...], o_high[...], LANES_BOTH)
    by_slot += dot(high_ref[...], o_low[...], LANES_BOTH)
    by_slot += dot(low_ref[...], o_high[...], LANES_BOTH)
    place = p_ref[...]
    cross = sum(dot(piece, place, PLAIN) for piece in split(by_slot, 3))
    out_ref[0:rows, :] = before_ref[0:rows, :] + cross
    means = sum(dot(piece, place, ROWS_BOTH) for piece in split(m_ref[...], 3))
    out_ref[rows : rows + SUB, :] = before_ref[rows : rows + SUB, :] + means


def cross_part(level_weight, skip, level_row, place, high, low, before, blocks, sums, number):
    rows, members = high.shape
    slots = blocks[0].shape[0]
    smem = pl.BlockSpec(memory_space=pltpu.SMEM)
    vmem = pl.BlockSpec(memory_space=pltpu.VMEM)
    held = len(number) * slots
    return pl.pallas_call(
        functools.partial(cross_kernel, number, slots),
        out_shape=jax.ShapeDtypeStruct(before.shape, F32),
        in_specs=[smem, smem] + [vmem] * (6 + len(blocks)),
        out_specs=vmem,
        scratch_shapes=[
            pltpu.VMEM((held, members), BF16),
            pltpu.VMEM((held, members), BF16),
            pltpu.VMEM((held, before.shape[1]), BF16),
            pltpu.VMEM((held, SUB), F32),
        ],
        compiler_params=pltpu.CompilerParams(vmem_limit_bytes=VMEM_LIMIT),
        cost_estimate=COST,
        name="cross_part",
    )(level_weight, skip, level_row, place, high, low, before, *blocks, sums)


def final_kernel(number, mem, width, weight_ref, taper_ref, sums_ref, *refs):
    parts, refs = refs[:mem], refs[mem:]
    blocks, (out_ref, w_high, w_low, chunk, sem) = refs[: len(number)], refs[len(number) :]
    rows = taper_ref.shape[0]
    members = out_ref.shape[1]
    me = lax.axis_index("rows")

    for n, block_ref in enumerate(blocks):
        length = block_ref.shape[0] // 2
        for side in range(2):
            at = pl.multiple_of((me ^ number[n] ^ side) * length, length)
            high, low = split(block_ref[side * length : (side + 1) * length, :], 2)
            w_high[pl.ds(at, length), :] = high
            w_low[pl.ds(at, length), :] = low

    cross = sum(ref[0:rows, :] for ref in parts)
    places = range(0, mem * SUB, SUB)
    counts = [sums_ref[at + LEVELS : at + SUB, :] for at in places]
    sums = [sums_ref[at : at + LEVELS, :] for at in places]
    total = sum(counts)
    mean = sum(sums) / total
    level = lax.broadcasted_iota(jnp.int32, (LEVELS, 1), 0)
    scale = by_level(level, [weight_ref[k] for k in range(LEVELS)]) / (total - 1.0)
    seen = [ref[rows : rows + LEVELS, :] for ref in parts]
    seen_counts = [c[:, 0:1] for c in counts]
    seen_mean = sum(c * s for c, s in zip(seen_counts, seen)) / total[:, 0:1]
    left, right = [], []
    for d in range(mem):
        left.append(scale * (sums[d] - counts[d] * mean))
        right.append(jnp.where(seen_counts[d] > 0.0, seen[d] - seen_mean, 0.0))
    left = split(jnp.concatenate(left, axis=0), 2)
    right = split(jnp.concatenate(right, axis=0), 2)
    cross += dot(left[0], right[0], ROWS_BOTH)
    cross += dot(left[0], right[1], ROWS_BOTH)
    cross += dot(left[1], right[0], ROWS_BOTH)
    t_high, t_low = split(cross * taper_ref[...], 2)

    copies = []
    for n in range(members // width):
        at = n * width
        out = dot(t_high, w_high[:, at : at + width], PLAIN)
        out += dot(t_high, w_low[:, at : at + width], PLAIN)
        out += dot(t_low, w_high[:, at : at + width], PLAIN)
        chunk[n, :, :] = out
        copies.append(pltpu.make_async_copy(chunk.at[n], out_ref.at[:, pl.ds(at, width)], sem.at[n]))
        copies[-1].start()
    for copy in copies:
        copy.wait()


def final(level_weight, parts, sums, taper, blocks, number):
    rows, observed = taper.shape
    members = blocks[0].shape[1]
    width = math.gcd(members, 256)
    smem = pl.BlockSpec(memory_space=pltpu.SMEM)
    vmem = pl.BlockSpec(memory_space=pltpu.VMEM)
    return pl.pallas_call(
        functools.partial(final_kernel, number, len(parts), width),
        out_shape=jax.ShapeDtypeStruct((rows, members), F32),
        in_specs=[smem] + [vmem] * (2 + len(parts) + len(blocks)),
        out_specs=pl.BlockSpec(memory_space=pl.ANY),
        scratch_shapes=[
            pltpu.VMEM((observed, members), BF16),
            pltpu.VMEM((observed, members), BF16),
            pltpu.VMEM((members // width, rows, width), F32),
            pltpu.SemaphoreType.DMA((members // width,)),
        ],
        compiler_params=pltpu.CompilerParams(vmem_limit_bytes=VMEM_LIMIT),
        cost_estimate=COST,
        name="final",
    )(level_weight, taper, sums, *parts, *blocks)


def across(x, axis, bits):
    count = lax.axis_size(axis)
    return lax.ppermute(x, axis, [(i, i ^ bits) for i in range(count)])


def gather_line(x, bits):
    blocks = {0: x}
    for bit in bits:
        for distance in list(blocks):
            blocks[distance ^ bit] = across(blocks[distance], "rows", bit)
    return blocks


def after(x, *others):
    return lax.optimization_barrier((x, *others))[0]


def on_device(state, member_level, level_weight, obs_row, state_coords, weights):
    groups = lax.axis_size("rows")
    radius = XCOL_DEV * groups
    row_count = state.shape[0]
    observed = obs_row.shape[0]
    bits = [1 << n for n in range(groups.bit_length() - 2, 0, -1)]
    slots = min(observed, 16 * (-(-2 * observed // groups) // 16))

    none = jnp.zeros((1,), jnp.int32)
    own = pick(obs_row, none, state, slots)
    level_row = after(member_level, own)[None, :]
    sums, high, low = center(level_row, after(state, own))
    all_sums = sums
    for n in range(lax.axis_size("mem").bit_length() - 1):
        all_sums = jnp.concatenate([all_sums, across(all_sums, "mem", 1 << n)])
        if n == 0:
            first_sums = all_sums

    line = gather_line(own, bits)
    other = {b ^ 1: across(after(x, first_sums) if b == 2 else x, "rows", 1) for b, x in line.items()}
    blocks = line | other
    early = [b for b in blocks if b < bits[0]]
    late = [b for b in blocks if b >= bits[0]]

    weights_far = across(after(weights, other[1]), "rows", 1)
    place, rounds, weights_pair = places(
        after(obs_row, other[early[-1]], all_sums), weights, weights_far, row_count, slots
    )

    def cross(skip, part, high, low, held, number):
        return cross_part(level_weight, skip, level_row, place, high, low, part, held, all_sums, number)

    def more(carry):
        return carry[0] < rounds[0]

    def another(carry):
        turn, part = carry
        skip = (turn * slots)[None]
        again = after(state, turn)
        block = pick(obs_row, skip, again, slots)
        _, high, low = center(level_row, again)
        parcels = [lax.all_gather(x, "rows", axis=0) for x in jnp.split(block, slots // 16)]
        every = jnp.concatenate(parcels, axis=1)
        me = lax.axis_index("rows")
        part = cross(skip, part, high, low, [every[me ^ b] for b in early + late], early + late)
        return turn + 1, part

    empty = jnp.zeros((row_count + SUB, observed), F32)
    _, part = lax.while_loop(more, another, (jnp.int32(1), after(empty, other[bits[0] ^ 1])))
    half = cross(none, part, high, low, [blocks[b] for b in early], early)
    part = cross(none, half, high, low, [blocks[b] for b in late], late)
    parts = [part] + [across(part, "mem", b) for b in range(1, lax.axis_size("mem"))]

    far_pair = across(weights_pair, "rows", bits[0])
    weights_line = gather_line(after(weights_pair, half), bits[1:])
    weights_line |= {b ^ bits[0]: x for b, x in gather_line(after(far_pair, part), bits[1:]).items()}
    taper = tapers(after(obs_row, part), state_coords, row_count, radius)
    return final(level_weight, parts, all_sums, taper, list(weights_line.values()), list(weights_line))


def solution(mesh):
    in_specs = (P("rows", "mem"), P("mem"), P(), P(), P(), P("rows", "mem"))
    out_specs = P("rows", "mem")
    return jax.shard_map(
        on_device, mesh=mesh, in_specs=in_specs, out_specs=out_specs, check_vma=False
    )
```

```python
import functools
import math

import jax
import jax.numpy as jnp
from jax import lax
from jax.experimental import pallas as pl
from jax.experimental.pallas import tpu as pltpu
from jax.sharding import PartitionSpec as P

LEVELS = 4
XCOL_DEV = 4
SUB = 8
VMEM_LIMIT = 48 * 1024 * 1024
COST = pl.CostEstimate(flops=1, bytes_accessed=1, transcendentals=0)
F32 = jnp.float32
BF16 = jnp.bfloat16
LANES_BOTH = (((1,), (1,)), ((), ()))
ROWS_BOTH = (((0,), (0,)), ((), ()))
PLAIN = (((1,), (0,)), ((), ()))


def dot(a, b, dims):
    return lax.dot_general(a, b, dims, preferred_element_type=F32)


def split(x, parts):
    pieces = []
    for _ in range(parts - 1):
        piece = x.astype(BF16)
        pieces.append(piece)
        x = x - piece.astype(F32)
    pieces.append(x.astype(BF16))
    return pieces


def level_onehot(level_row):
    levels = lax.broadcasted_iota(jnp.int32, (SUB, level_row.shape[1]), 0)
    return (level_row == levels).astype(F32)


def by_level(level_row, columns):
    picked = jnp.where(level_row == 1, columns[1], columns[0])
    for level in range(2, LEVELS):
        picked = jnp.where(level_row == level, columns[level], picked)
    return picked


def pick_kernel(obs_ref, skip_ref, weights_ref, state_ref, out_ref, both_ref, list_ref, held_ref, sem):
    rows = state_ref.shape[0]
    slots, members = out_ref.shape
    row_first = lax.axis_index("rows") * rows
    skip = skip_ref[0]
    copy = pltpu.make_async_copy(state_ref, held_ref, sem)
    copy.start()
    both_ref[slots:, :] = weights_ref[...]

    def visit(j, rank):
        row = obs_ref[j] - row_first
        list_ref[rank] = row
        return rank + ((row >= 0) & (row < rows)).astype(jnp.int32)

    total = lax.fori_loop(0, obs_ref.shape[0], visit, 0, unroll=8)
    held = jnp.clip(total - skip, 0, slots)
    copy.wait()

    for slot in range(slots):
        row = jnp.clip(list_ref[skip + slot], 0, rows - 1)
        value = jnp.where(slot < held, held_ref[pl.ds(row, 1), :], 0.0)
        out_ref[slot : slot + 1, :] = value
        both_ref[slot : slot + 1, :] = value


def pick(obs_row, skip, weights, state, slots):
    members = state.shape[1]
    smem = pl.BlockSpec(memory_space=pltpu.SMEM)
    vmem = pl.BlockSpec(memory_space=pltpu.VMEM)
    return pl.pallas_call(
        pick_kernel,
        out_shape=(
            jax.ShapeDtypeStruct((slots, members), F32),
            jax.ShapeDtypeStruct((slots + weights.shape[0], members), F32),
        ),
        in_specs=[smem, smem, vmem, pl.BlockSpec(memory_space=pl.ANY)],
        out_specs=(vmem, vmem),
        scratch_shapes=[
            pltpu.SMEM((obs_row.shape[0] + slots + 1,), jnp.int32),
            pltpu.VMEM(state.shape, F32),
            pltpu.SemaphoreType.DMA(()),
        ],
        compiler_params=pltpu.CompilerParams(vmem_limit_bytes=VMEM_LIMIT),
        cost_estimate=COST,
        name="pick",
    )(obs_row, skip, weights, state)


def center_kernel(level_ref, state_ref, sums_ref, high_ref, low_ref):
    level_row = level_ref[...]
    onehot = level_onehot(level_row)
    counts = jnp.sum(onehot, axis=1, keepdims=True)
    state = state_ref[...]
    hot = onehot.astype(BF16)
    sums = sum(dot(hot, piece, LANES_BOTH) for piece in split(state, 3))
    sums_ref[0:LEVELS, :] = sums[0:LEVELS, :]
    sums_ref[LEVELS:SUB, :] = jnp.broadcast_to(counts[0:LEVELS, :], (LEVELS, sums.shape[1]))
    means = jnp.transpose(sums / jnp.maximum(counts, 1.0))
    columns = [means[:, level : level + 1] for level in range(LEVELS)]
    high, low = split(state - by_level(level_row, columns), 2)
    high_ref[...] = high
    low_ref[...] = low


def center(level_row, state):
    rows, members = state.shape
    tall = math.gcd(rows, 128)
    return pl.pallas_call(
        center_kernel,
        out_shape=(
            jax.ShapeDtypeStruct((SUB, rows), F32),
            jax.ShapeDtypeStruct((rows, members), BF16),
            jax.ShapeDtypeStruct((rows, members), BF16),
        ),
        grid=(rows // tall,),
        in_specs=[
            pl.BlockSpec((1, members), lambda i: (0, 0)),
            pl.BlockSpec((tall, members), lambda i: (i, 0)),
        ],
        out_specs=(
            pl.BlockSpec((SUB, tall), lambda i: (0, i)),
            pl.BlockSpec((tall, members), lambda i: (i, 0)),
            pl.BlockSpec((tall, members), lambda i: (i, 0)),
        ),
        compiler_params=pltpu.CompilerParams(vmem_limit_bytes=VMEM_LIMIT),
        cost_estimate=COST,
        name="center",
    )(level_row, state)


def pair_kernel(near_ref, far_ref, pair_ref):
    length = near_ref.shape[0]
    pair_ref[0:length, :] = near_ref[...]
    pair_ref[length : 2 * length, :] = far_ref[far_ref.shape[0] - length :, :]


def pairs(near, far):
    length, members = near.shape
    vmem = pl.BlockSpec(memory_space=pltpu.VMEM)
    return pl.pallas_call(
        pair_kernel,
        out_shape=jax.ShapeDtypeStruct((2 * length, members), F32),
        in_specs=[vmem, vmem],
        out_specs=vmem,
        compiler_params=pltpu.CompilerParams(vmem_limit_bytes=VMEM_LIMIT),
        cost_estimate=COST,
        name="pairs",
    )(near, far)


def place_kernel(slots, rows, obs_ref, place_ref, rounds_ref, zero_ref):
    observed = obs_ref.shape[1]
    zero_ref[...] = jnp.zeros_like(zero_ref)
    owner = lax.div(obs_ref[...], jnp.int32(rows))
    owner_row = owner.astype(F32)
    owner_down = jnp.transpose(jnp.broadcast_to(owner_row, (SUB, observed)))[:, 0:1]
    j_down = lax.broadcasted_iota(jnp.int32, (observed, observed), 0)
    j_row = lax.broadcasted_iota(jnp.int32, (observed, observed), 1)
    earlier = (owner_down == owner_row) & (j_down < j_row)
    rank = jnp.sum(earlier.astype(F32), axis=0, keepdims=True).astype(jnp.int32)
    place_ref[0:1, :] = owner
    place_ref[1:2, :] = rank
    place_ref[2:SUB, :] = jnp.zeros((SUB - 2, observed), jnp.int32)
    rounds_ref[0] = lax.div(jnp.max(rank), jnp.int32(slots)) + 1


def places(obs_row, rows, slots):
    observed = obs_row.shape[0]
    vmem = pl.BlockSpec(memory_space=pltpu.VMEM)
    smem = pl.BlockSpec(memory_space=pltpu.SMEM)
    return pl.pallas_call(
        functools.partial(place_kernel, slots, rows),
        out_shape=(
            jax.ShapeDtypeStruct((SUB, observed), jnp.int32),
            jax.ShapeDtypeStruct((1,), jnp.int32),
            jax.ShapeDtypeStruct((rows + SUB, observed), F32),
        ),
        in_specs=[vmem],
        out_specs=(vmem, smem, vmem),
        compiler_params=pltpu.CompilerParams(vmem_limit_bytes=VMEM_LIMIT),
        name="places",
    )(obs_row[None, :])


def taper_kernel(radius, obs_ref, coords_ref, taper_ref):
    rows, observed = taper_ref.shape
    total = coords_ref.shape[1]
    chunk = math.gcd(total, 256)
    obs = obs_ref[...]

    def look(n, seen):
        at = pl.multiple_of(n * chunk, chunk)
        row = lax.broadcasted_iota(jnp.int32, (chunk, observed), 0) + at
        coords = coords_ref[:, pl.ds(at, chunk)].astype(F32).astype(BF16)
        return seen + dot(coords, (row == obs).astype(BF16), PLAIN)

    seen = lax.fori_loop(0, total // chunk, look, jnp.zeros((2, observed), F32), unroll=min(8, total // chunk))
    first = pl.multiple_of(lax.axis_index("rows") * rows, rows)
    own = coords_ref[:, pl.ds(first, rows)].astype(F32)
    own_x = jnp.transpose(jnp.broadcast_to(own[0:1, :], (SUB, rows)))[:, 0:1]
    own_y = jnp.transpose(jnp.broadcast_to(own[1:2, :], (SUB, rows)))[:, 0:1]
    offset_x = own_x - seen[0:1, :]
    offset_y = own_y - seen[1:2, :]
    distance = offset_x * offset_x + offset_y * offset_y
    reach = jnp.maximum(0.0, 1.0 - distance / float(radius * radius))
    taper_ref[...] = reach * reach


def tapers(obs_row, state_coords, rows, radius):
    vmem = pl.BlockSpec(memory_space=pltpu.VMEM)
    return pl.pallas_call(
        functools.partial(taper_kernel, radius),
        out_shape=jax.ShapeDtypeStruct((rows, obs_row.shape[0]), F32),
        in_specs=[vmem, vmem],
        out_specs=vmem,
        compiler_params=pltpu.CompilerParams(vmem_limit_bytes=VMEM_LIMIT),
        name="tapers",
    )(obs_row[None, :], state_coords)


def cross_kernel(number, slots, weight_ref, skip_ref, level_ref, place_ref, high_ref, low_ref, before_ref, *refs):
    blocks, (sums_ref, out_ref, o_high, o_low, p_ref, m_ref) = refs[: len(number)], refs[len(number) :]
    rows = high_ref.shape[0]
    me = lax.axis_index("rows")
    skip = skip_ref[0]
    level_row = level_ref[...]
    onehot = level_onehot(level_row)
    counts = jnp.maximum(jnp.sum(onehot, axis=1, keepdims=True), 1.0)
    total = sum(
        sums_ref[at + LEVELS : at + SUB, 0:128] for at in range(0, sums_ref.shape[0], SUB)
    )
    scales = [weight_ref[level] / (total[level, 0] - 1.0) for level in range(LEVELS)]
    member_scale = by_level(level_row, scales)
    owner, rank = place_ref[0:1, :], place_ref[1:2, :]
    padded = o_high.shape[0] // len(number)
    m_ref[...] = jnp.zeros_like(m_ref)
    for n, block_ref in enumerate(blocks):
        at = n * padded
        block = block_ref[0:slots, :]
        columns = []
        for level in range(LEVELS):
            member = jnp.where(level_row == level, block, 0.0)
            columns.append(jnp.sum(member, axis=1, keepdims=True) / counts[level : level + 1, :])
            m_ref[at : at + slots, level : level + 1] = columns[level]
        high, low = split((block - by_level(level_row, columns)) * member_scale, 2)
        o_high[at : at + slots, :] = high
        o_low[at : at + slots, :] = low
        slot = lax.broadcasted_iota(jnp.int32, (slots, owner.shape[1]), 0)
        hit = (owner == (me ^ number[n])) & (rank - skip == slot)
        p_ref[at : at + slots, :] = hit.astype(BF16)
    by_slot = dot(high_ref[...], o_high[...], LANES_BOTH)
    by_slot += dot(high_ref[...], o_low[...], LANES_BOTH)
    by_slot += dot(low_ref[...], o_high[...], LANES_BOTH)
    place = p_ref[...]
    cross = sum(dot(piece, place, PLAIN) for piece in split(by_slot, 3))
    out_ref[0:rows, :] = before_ref[0:rows, :] + cross
    means = sum(dot(piece, place, ROWS_BOTH) for piece in split(m_ref[...], 3))
    out_ref[rows : rows + SUB, :] = before_ref[rows : rows + SUB, :] + means


def cross_part(level_weight, skip, level_row, place, high, low, before, blocks, sums, slots, number):
    rows, members = high.shape
    smem = pl.BlockSpec(memory_space=pltpu.SMEM)
    vmem = pl.BlockSpec(memory_space=pltpu.VMEM)
    held = len(number) * slots
    return pl.pallas_call(
        functools.partial(cross_kernel, number, slots),
        out_shape=jax.ShapeDtypeStruct(before.shape, F32),
        in_specs=[smem, smem] + [vmem] * (6 + len(blocks)),
        out_specs=vmem,
        scratch_shapes=[
            pltpu.VMEM((held, members), BF16),
            pltpu.VMEM((held, members), BF16),
            pltpu.VMEM((held, before.shape[1]), BF16),
            pltpu.VMEM((held, SUB), F32),
        ],
        compiler_params=pltpu.CompilerParams(vmem_limit_bytes=VMEM_LIMIT),
        cost_estimate=COST,
        name="cross_part",
    )(level_weight, skip, level_row, place, high, low, before, *blocks, sums)


def final_kernel(number, mem, width, weight_ref, taper_ref, sums_ref, *refs):
    parts, refs = refs[:mem], refs[mem:]
    blocks, (out_ref, w_high, w_low, chunk, sem) = refs[: len(number)], refs[len(number) :]
    rows = taper_ref.shape[0]
    members = out_ref.shape[1]
    me = lax.axis_index("rows")

    for n, block_ref in enumerate(blocks):
        length = block_ref.shape[0] // 2
        for side in range(2):
            at = pl.multiple_of((me ^ number[n] ^ side) * length, length)
            high, low = split(block_ref[side * length : (side + 1) * length, :], 2)
            w_high[pl.ds(at, length), :] = high
            w_low[pl.ds(at, length), :] = low

    cross = sum(ref[0:rows, :] for ref in parts)
    places = range(0, mem * SUB, SUB)
    counts = [sums_ref[at + LEVELS : at + SUB, :] for at in places]
    sums = [sums_ref[at : at + LEVELS, :] for at in places]
    total = sum(counts)
    mean = sum(sums) / total
    level = lax.broadcasted_iota(jnp.int32, (LEVELS, 1), 0)
    scale = by_level(level, [weight_ref[k] for k in range(LEVELS)]) / (total - 1.0)
    seen = [ref[rows : rows + LEVELS, :] for ref in parts]
    seen_counts = [c[:, 0:1] for c in counts]
    seen_mean = sum(c * s for c, s in zip(seen_counts, seen)) / total[:, 0:1]
    left, right = [], []
    for d in range(mem):
        left.append(scale * (sums[d] - counts[d] * mean))
        right.append(jnp.where(seen_counts[d] > 0.0, seen[d] - seen_mean, 0.0))
    left = split(jnp.concatenate(left, axis=0), 2)
    right = split(jnp.concatenate(right, axis=0), 2)
    cross += dot(left[0], right[0], ROWS_BOTH)
    cross += dot(left[0], right[1], ROWS_BOTH)
    cross += dot(left[1], right[0], ROWS_BOTH)
    t_high, t_low = split(cross * taper_ref[...], 2)

    copies = []
    for n in range(members // width):
        at = n * width
        out = dot(t_high, w_high[:, at : at + width], PLAIN)
        out += dot(t_high, w_low[:, at : at + width], PLAIN)
        out += dot(t_low, w_high[:, at : at + width], PLAIN)
        chunk[n, :, :] = out
        copies.append(pltpu.make_async_copy(chunk.at[n], out_ref.at[:, pl.ds(at, width)], sem.at[n]))
        copies[-1].start()
    for copy in copies:
        copy.wait()


def final(level_weight, parts, sums, taper, blocks, number):
    rows, observed = taper.shape
    members = blocks[0].shape[1]
    width = math.gcd(members, 256)
    smem = pl.BlockSpec(memory_space=pltpu.SMEM)
    vmem = pl.BlockSpec(memory_space=pltpu.VMEM)
    return pl.pallas_call(
        functools.partial(final_kernel, number, len(parts), width),
        out_shape=jax.ShapeDtypeStruct((rows, members), F32),
        in_specs=[smem] + [vmem] * (2 + len(parts) + len(blocks)),
        out_specs=pl.BlockSpec(memory_space=pl.ANY),
        scratch_shapes=[
            pltpu.VMEM((observed, members), BF16),
            pltpu.VMEM((observed, members), BF16),
            pltpu.VMEM((members // width, rows, width), F32),
            pltpu.SemaphoreType.DMA((members // width,)),
        ],
        compiler_params=pltpu.CompilerParams(vmem_limit_bytes=VMEM_LIMIT),
        cost_estimate=COST,
        name="final",
    )(level_weight, taper, sums, *parts, *blocks)


def across(x, axis, bits):
    count = lax.axis_size(axis)
    return lax.ppermute(x, axis, [(i, i ^ bits) for i in range(count)])


def gather_line(x, bits):
    blocks = {0: x}
    for bit in bits:
        for distance in list(blocks):
            blocks[distance ^ bit] = across(blocks[distance], "rows", bit)
    return blocks


def after(x, *others):
    return lax.optimization_barrier((x, *others))[0]


def on_device(state, member_level, level_weight, obs_row, state_coords, weights):
    groups = lax.axis_size("rows")
    radius = XCOL_DEV * groups
    row_count = state.shape[0]
    observed = obs_row.shape[0]
    bits = [1 << n for n in range(groups.bit_length() - 2, 0, -1)]
    slots = min(observed, 16 * (-(-2 * observed // groups) // 16))

    none = jnp.zeros((1,), jnp.int32)
    own, own_both = pick(obs_row, none, weights, state, slots)
    level_row = after(member_level, own)[None, :]
    sums, high, low = center(level_row, after(state, own))
    near_far = across(own_both, "rows", 1)
    near_sums = after(sums, near_far)
    near_sums = jnp.concatenate([near_sums, across(near_sums, "mem", 1)])
    place, rounds, empty = places(after(obs_row, own), row_count, slots)
    first_far = across(own, "rows", bits[0])
    line = gather_line(own, bits[1:])
    line |= {
        b ^ bits[0]: x for b, x in gather_line(after(first_far, near_sums, place), bits[1:]).items()
    }
    forward = {b: x for b, x in line.items()}
    other = {b ^ 1: across(x, "rows", 1) if b else near_far for b, x in forward.items()}
    all_sums = near_sums
    for n in range(1, lax.axis_size("mem").bit_length() - 1):
        all_sums = jnp.concatenate([all_sums, across(all_sums, "mem", 1 << n)])
    blocks = line | other
    early = [b for b in blocks if b < bits[0]]
    late = [b for b in blocks if b >= bits[0]]

    weights_pair = pairs(weights, after(other[1], all_sums))

    def cross(skip, part, high, low, held, number):
        return cross_part(level_weight, skip, level_row, place, high, low, part, held, all_sums, slots, number)

    def more(carry):
        return carry[0] < rounds[0]

    def another(carry):
        turn, part = carry
        skip = (turn * slots)[None]
        again = after(state, turn)
        block, _ = pick(obs_row, skip, weights, again, slots)
        _, high, low = center(level_row, again)
        parcels = [lax.all_gather(x, "rows", axis=0) for x in jnp.split(block, slots // 16)]
        every = jnp.concatenate(parcels, axis=1)
        me = lax.axis_index("rows")
        part = cross(skip, part, high, low, [every[me ^ b] for b in early + late], early + late)
        return turn + 1, part

    _, looped = lax.while_loop(more, another, (jnp.int32(1), empty))
    half = cross(none, looped, high, low, [blocks[b] for b in early], early)
    part = cross(none, half, high, low, [blocks[b] for b in late], late)
    parts = [part] + [across(part, "mem", b) for b in range(1, lax.axis_size("mem"))]

    far_pair = across(after(weights_pair, looped), "rows", bits[0])
    weights_line = gather_line(after(weights_pair, half), bits[1:])
    weights_line |= {b ^ bits[0]: x for b, x in gather_line(after(far_pair, part), bits[1:]).items()}
    taper = tapers(after(obs_row, part), state_coords, row_count, radius)
    return final(level_weight, parts, all_sums, taper, list(weights_line.values()), list(weights_line))


def solution(mesh):
    in_specs = (P("rows", "mem"), P("mem"), P(), P(), P(), P("rows", "mem"))
    out_specs = P("rows", "mem")
    return jax.shard_map(
        on_device, mesh=mesh, in_specs=in_specs, out_specs=out_specs, check_vma=False
    )
```

```python
import functools
import math

import jax
import jax.numpy as jnp
from jax import lax
from jax.experimental import pallas as pl
from jax.experimental.pallas import tpu as pltpu
from jax.sharding import PartitionSpec as P

LEVELS = 4
XCOL_DEV = 4
SUB = 8
VMEM_LIMIT = 48 * 1024 * 1024
COST = pl.CostEstimate(flops=1, bytes_accessed=1, transcendentals=0)
F32 = jnp.float32
BF16 = jnp.bfloat16
LANES_BOTH = (((1,), (1,)), ((), ()))
ROWS_BOTH = (((0,), (0,)), ((), ()))
PLAIN = (((1,), (0,)), ((), ()))


def dot(a, b, dims):
    return lax.dot_general(a, b, dims, preferred_element_type=F32)


def split(x, parts):
    pieces = []
    for _ in range(parts - 1):
        piece = x.astype(BF16)
        pieces.append(piece)
        x = x - piece.astype(F32)
    pieces.append(x.astype(BF16))
    return pieces


def packing(slots, members):
    lanes = members // 128
    full = slots - slots % SUB
    pieces = [(n * full, full, 0, n * 128) for n in range(lanes)] if full else []
    tail = slots - full
    if tail:
        pieces += [(lanes * full + n * tail, tail, full, n * 128) for n in range(lanes)]
    return pieces


def level_onehot(level_row):
    levels = lax.broadcasted_iota(jnp.int32, (SUB, level_row.shape[1]), 0)
    return (level_row == levels).astype(F32)


def by_level(level_row, columns):
    picked = jnp.where(level_row == 1, columns[1], columns[0])
    for level in range(2, LEVELS):
        picked = jnp.where(level_row == level, columns[level], picked)
    return picked


def pick_kernel(slots, obs_ref, skip_ref, state_ref, out_ref, list_ref, held_ref, row_ref, sem):
    rows, members = state_ref.shape
    row_first = lax.axis_index("rows") * rows
    skip = skip_ref[0]
    copy = pltpu.make_async_copy(state_ref, held_ref, sem)
    copy.start()

    def visit(j, rank):
        row = obs_ref[j] - row_first
        list_ref[rank] = row
        return rank + ((row >= 0) & (row < rows)).astype(jnp.int32)

    total = lax.fori_loop(0, obs_ref.shape[0], visit, 0, unroll=8)
    held = jnp.clip(total - skip, 0, slots)
    copy.wait()

    for slot in range(slots):
        row = jnp.clip(list_ref[skip + slot], 0, rows - 1)
        value = jnp.where(slot < held, held_ref[pl.ds(row, 1), :], 0.0)
        row_ref[slot : slot + 1, :] = value
    for at, tall, row, lane in packing(slots, members):
        out_ref[at : at + tall, :] = row_ref[row : row + tall, lane : lane + 128]


def pick(obs_row, skip, state, slots):
    smem = pl.BlockSpec(memory_space=pltpu.SMEM)
    return pl.pallas_call(
        functools.partial(pick_kernel, slots),
        out_shape=jax.ShapeDtypeStruct((slots * (state.shape[1] // 128), 128), F32),
        in_specs=[smem, smem, pl.BlockSpec(memory_space=pl.ANY)],
        out_specs=pl.BlockSpec(memory_space=pltpu.VMEM),
        scratch_shapes=[
            pltpu.SMEM((obs_row.shape[0] + slots + 1,), jnp.int32),
            pltpu.VMEM(state.shape, F32),
            pltpu.VMEM((-(-slots // SUB) * SUB, state.shape[1]), F32),
            pltpu.SemaphoreType.DMA(()),
        ],
        compiler_params=pltpu.CompilerParams(vmem_limit_bytes=VMEM_LIMIT),
        cost_estimate=COST,
        name="pick",
    )(obs_row, skip, state)


def place(slots, rows, obs_ref, place_ref, rounds_ref):
    observed = obs_ref.shape[1]
    owner = lax.div(obs_ref[...], jnp.int32(rows))
    owner_row = owner.astype(F32)
    owner_down = jnp.transpose(jnp.broadcast_to(owner_row, (SUB, observed)))[:, 0:1]
    j_down = lax.broadcasted_iota(jnp.int32, (observed, observed), 0)
    j_row = lax.broadcasted_iota(jnp.int32, (observed, observed), 1)
    earlier = (owner_down == owner_row) & (j_down < j_row)
    rank = jnp.sum(earlier.astype(F32), axis=0, keepdims=True).astype(jnp.int32)
    place_ref[0:1, :] = owner
    place_ref[1:2, :] = rank
    place_ref[2:SUB, :] = jnp.zeros((SUB - 2, observed), jnp.int32)
    rounds_ref[0] = lax.div(jnp.max(rank), jnp.int32(slots)) + 1


def center_kernel(
    slots, rows, obs_ref, own_ref, weights_ref, level_ref, state_ref, sums_ref, high_ref, low_ref,
    both_ref, place_ref, zero_ref, rounds_ref,
):
    @pl.when(pl.program_id(0) == 0)
    def _():
        held, (length, members) = own_ref.shape[0], weights_ref.shape
        both_ref[0:held, :] = own_ref[...]
        for at, tall, row, lane in packing(length, members):
            both_ref[held + at : held + at + tall, :] = weights_ref[row : row + tall, lane : lane + 128]
        place(slots, rows, obs_ref, place_ref, rounds_ref)
        zero_ref[...] = jnp.zeros_like(zero_ref)

    level_row = level_ref[...]
    onehot = level_onehot(level_row)
    counts = jnp.sum(onehot, axis=1, keepdims=True)
    state = state_ref[...]
    hot = onehot.astype(BF16)
    sums = sum(dot(hot, piece, LANES_BOTH) for piece in split(state, 3))
    sums_ref[0:LEVELS, :] = sums[0:LEVELS, :]
    sums_ref[LEVELS:SUB, :] = jnp.broadcast_to(counts[0:LEVELS, :], (LEVELS, sums.shape[1]))
    means = jnp.transpose(sums / jnp.maximum(counts, 1.0))
    columns = [means[:, level : level + 1] for level in range(LEVELS)]
    high, low = split(state - by_level(level_row, columns), 2)
    high_ref[...] = high
    low_ref[...] = low


def center(obs_row, own, weights, level_row, state):
    rows, members = state.shape
    observed = obs_row.shape[0]
    slots = own.shape[0] // (members // 128)
    tall = math.gcd(rows, 128)
    whole = lambda *shape: pl.BlockSpec(shape, lambda i: (0, 0))
    both = (own.shape[0] + weights.shape[0] * (members // 128), 128)
    return pl.pallas_call(
        functools.partial(center_kernel, slots, rows),
        out_shape=(
            jax.ShapeDtypeStruct((SUB, rows), F32),
            jax.ShapeDtypeStruct((rows, members), BF16),
            jax.ShapeDtypeStruct((rows, members), BF16),
            jax.ShapeDtypeStruct(both, F32),
            jax.ShapeDtypeStruct((SUB, observed), jnp.int32),
            jax.ShapeDtypeStruct((rows + SUB, observed), F32),
            jax.ShapeDtypeStruct((1,), jnp.int32),
        ),
        grid=(rows // tall,),
        in_specs=[
            whole(1, observed),
            whole(*own.shape),
            whole(*weights.shape),
            whole(1, members),
            pl.BlockSpec((tall, members), lambda i: (i, 0)),
        ],
        out_specs=(
            pl.BlockSpec((SUB, tall), lambda i: (0, i)),
            pl.BlockSpec((tall, members), lambda i: (i, 0)),
            pl.BlockSpec((tall, members), lambda i: (i, 0)),
            whole(*both),
            whole(SUB, observed),
            whole(rows + SUB, observed),
            pl.BlockSpec(memory_space=pltpu.SMEM),
        ),
        compiler_params=pltpu.CompilerParams(vmem_limit_bytes=VMEM_LIMIT),
        cost_estimate=COST,
        name="center",
    )(obs_row[None, :], own, weights, level_row, state)


def pair_kernel(near_ref, far_ref, pair_ref):
    length = near_ref.shape[0]
    pair_ref[0:length, :] = near_ref[...]
    members = near_ref.shape[1]
    held = far_ref.shape[0] - length * (members // 128)
    for at, tall, row, lane in packing(length, members):
        pair_ref[length + row : length + row + tall, lane : lane + 128] = far_ref[held + at : held + at + tall, :]


def pairs(near, far):
    length, members = near.shape
    vmem = pl.BlockSpec(memory_space=pltpu.VMEM)
    return pl.pallas_call(
        pair_kernel,
        out_shape=jax.ShapeDtypeStruct((2 * length, members), F32),
        in_specs=[vmem, vmem],
        out_specs=vmem,
        compiler_params=pltpu.CompilerParams(vmem_limit_bytes=VMEM_LIMIT),
        cost_estimate=COST,
        name="pairs",
    )(near, far)


def taper_kernel(radius, obs_ref, coords_ref, taper_ref):
    rows, observed = taper_ref.shape
    total = coords_ref.shape[1]
    chunk = math.gcd(total, 256)
    obs = obs_ref[...]

    def look(n, seen):
        at = pl.multiple_of(n * chunk, chunk)
        row = lax.broadcasted_iota(jnp.int32, (chunk, observed), 0) + at
        coords = coords_ref[:, pl.ds(at, chunk)].astype(F32).astype(BF16)
        return seen + dot(coords, (row == obs).astype(BF16), PLAIN)

    seen = lax.fori_loop(0, total // chunk, look, jnp.zeros((2, observed), F32), unroll=min(8, total // chunk))
    first = pl.multiple_of(lax.axis_index("rows") * rows, rows)
    own = coords_ref[:, pl.ds(first, rows)].astype(F32)
    own_x = jnp.transpose(jnp.broadcast_to(own[0:1, :], (SUB, rows)))[:, 0:1]
    own_y = jnp.transpose(jnp.broadcast_to(own[1:2, :], (SUB, rows)))[:, 0:1]
    offset_x = own_x - seen[0:1, :]
    offset_y = own_y - seen[1:2, :]
    distance = offset_x * offset_x + offset_y * offset_y
    reach = jnp.maximum(0.0, 1.0 - distance / float(radius * radius))
    taper_ref[...] = reach * reach


def tapers(obs_row, state_coords, rows, radius):
    vmem = pl.BlockSpec(memory_space=pltpu.VMEM)
    return pl.pallas_call(
        functools.partial(taper_kernel, radius),
        out_shape=jax.ShapeDtypeStruct((rows, obs_row.shape[0]), F32),
        in_specs=[vmem, vmem],
        out_specs=vmem,
        compiler_params=pltpu.CompilerParams(vmem_limit_bytes=VMEM_LIMIT),
        name="tapers",
    )(obs_row[None, :], state_coords)


def cross_kernel(number, slots, weight_ref, skip_ref, level_ref, place_ref, high_ref, low_ref, before_ref, *refs):
    blocks, (sums_ref, out_ref, o_high, o_low, p_ref, m_ref, raw_ref) = refs[: len(number)], refs[len(number) :]
    rows = high_ref.shape[0]
    me = lax.axis_index("rows")
    skip = skip_ref[0]
    level_row = level_ref[...]
    onehot = level_onehot(level_row)
    counts = jnp.maximum(jnp.sum(onehot, axis=1, keepdims=True), 1.0)
    total = sum(
        sums_ref[at + LEVELS : at + SUB, 0:128] for at in range(0, sums_ref.shape[0], SUB)
    )
    scales = [weight_ref[level] / (total[level, 0] - 1.0) for level in range(LEVELS)]
    member_scale = by_level(level_row, scales)
    owner, rank = place_ref[0:1, :], place_ref[1:2, :]
    padded = o_high.shape[0] // len(number)
    m_ref[...] = jnp.zeros_like(m_ref)
    for n, block_ref in enumerate(blocks):
        at = n * padded
        raw_ref[at + padded - SUB : at + padded, :] = jnp.zeros((SUB, raw_ref.shape[1]), F32)
        for start, tall, row, lane in packing(slots, raw_ref.shape[1]):
            raw_ref[at + row : at + row + tall, lane : lane + 128] = block_ref[start : start + tall, :]
        block = raw_ref[at : at + padded, :]
        columns = []
        for level in range(LEVELS):
            member = jnp.where(level_row == level, block, 0.0)
            columns.append(jnp.sum(member, axis=1, keepdims=True) / counts[level : level + 1, :])
            m_ref[at : at + padded, level : level + 1] = columns[level]
        high, low = split((block - by_level(level_row, columns)) * member_scale, 2)
        o_high[at : at + padded, :] = high
        o_low[at : at + padded, :] = low
        slot = lax.broadcasted_iota(jnp.int32, (padded, owner.shape[1]), 0)
        hit = (owner == (me ^ number[n])) & (rank - skip == slot) & (slot < slots)
        p_ref[at : at + padded, :] = hit.astype(BF16)
    by_slot = dot(high_ref[...], o_high[...], LANES_BOTH)
    by_slot += dot(high_ref[...], o_low[...], LANES_BOTH)
    by_slot += dot(low_ref[...], o_high[...], LANES_BOTH)
    place = p_ref[...]
    cross = sum(dot(piece, place, PLAIN) for piece in split(by_slot, 3))
    out_ref[0:rows, :] = before_ref[0:rows, :] + cross
    means = sum(dot(piece, place, ROWS_BOTH) for piece in split(m_ref[...], 3))
    out_ref[rows : rows + SUB, :] = before_ref[rows : rows + SUB, :] + means


def cross_part(level_weight, skip, level_row, place, high, low, before, blocks, sums, slots, number):
    rows, members = high.shape
    smem = pl.BlockSpec(memory_space=pltpu.SMEM)
    vmem = pl.BlockSpec(memory_space=pltpu.VMEM)
    held = len(number) * -(-slots // 16) * 16
    return pl.pallas_call(
        functools.partial(cross_kernel, number, slots),
        out_shape=jax.ShapeDtypeStruct(before.shape, F32),
        in_specs=[smem, smem] + [vmem] * (6 + len(blocks)),
        out_specs=vmem,
        scratch_shapes=[
            pltpu.VMEM((held, members), BF16),
            pltpu.VMEM((held, members), BF16),
            pltpu.VMEM((held, before.shape[1]), BF16),
            pltpu.VMEM((held, SUB), F32),
            pltpu.VMEM((held, members), F32),
        ],
        compiler_params=pltpu.CompilerParams(vmem_limit_bytes=VMEM_LIMIT),
        cost_estimate=COST,
        name="cross_part",
    )(level_weight, skip, level_row, place, high, low, before, *blocks, sums)


def final_kernel(number, mem, width, weight_ref, taper_ref, sums_ref, *refs):
    parts, refs = refs[:mem], refs[mem:]
    blocks, (out_ref, w_high, w_low, chunk, sem) = refs[: len(number)], refs[len(number) :]
    rows = taper_ref.shape[0]
    members = out_ref.shape[1]
    me = lax.axis_index("rows")

    for n, block_ref in enumerate(blocks):
        length = block_ref.shape[0] // 2
        for side in range(2):
            at = pl.multiple_of((me ^ number[n] ^ side) * length, length)
            high, low = split(block_ref[side * length : (side + 1) * length, :], 2)
            w_high[pl.ds(at, length), :] = high
            w_low[pl.ds(at, length), :] = low

    cross = sum(ref[0:rows, :] for ref in parts)
    places = range(0, mem * SUB, SUB)
    counts = [sums_ref[at + LEVELS : at + SUB, :] for at in places]
    sums = [sums_ref[at : at + LEVELS, :] for at in places]
    total = sum(counts)
    mean = sum(sums) / total
    level = lax.broadcasted_iota(jnp.int32, (LEVELS, 1), 0)
    scale = by_level(level, [weight_ref[k] for k in range(LEVELS)]) / (total - 1.0)
    seen = [ref[rows : rows + LEVELS, :] for ref in parts]
    seen_counts = [c[:, 0:1] for c in counts]
    seen_mean = sum(c * s for c, s in zip(seen_counts, seen)) / total[:, 0:1]
    left, right = [], []
    for d in range(mem):
        left.append(scale * (sums[d] - counts[d] * mean))
        right.append(jnp.where(seen_counts[d] > 0.0, seen[d] - seen_mean, 0.0))
    left = split(jnp.concatenate(left, axis=0), 2)
    right = split(jnp.concatenate(right, axis=0), 2)
    cross += dot(left[0], right[0], ROWS_BOTH)
    cross += dot(left[0], right[1], ROWS_BOTH)
    cross += dot(left[1], right[0], ROWS_BOTH)
    t_high, t_low = split(cross * taper_ref[...], 2)

    copies = []
    for n in range(members // width):
        at = n * width
        out = dot(t_high, w_high[:, at : at + width], PLAIN)
        out += dot(t_high, w_low[:, at : at + width], PLAIN)
        out += dot(t_low, w_high[:, at : at + width], PLAIN)
        chunk[n, :, :] = out
        copies.append(pltpu.make_async_copy(chunk.at[n], out_ref.at[:, pl.ds(at, width)], sem.at[n]))
        copies[-1].start()
    for copy in copies:
        copy.wait()


def final(level_weight, parts, sums, taper, blocks, number):
    rows, observed = taper.shape
    members = blocks[0].shape[1]
    width = math.gcd(members, 256)
    smem = pl.BlockSpec(memory_space=pltpu.SMEM)
    vmem = pl.BlockSpec(memory_space=pltpu.VMEM)
    return pl.pallas_call(
        functools.partial(final_kernel, number, len(parts), width),
        out_shape=jax.ShapeDtypeStruct((rows, members), F32),
        in_specs=[smem] + [vmem] * (2 + len(parts) + len(blocks)),
        out_specs=pl.BlockSpec(memory_space=pl.ANY),
        scratch_shapes=[
            pltpu.VMEM((observed, members), BF16),
            pltpu.VMEM((observed, members), BF16),
            pltpu.VMEM((members // width, rows, width), F32),
            pltpu.SemaphoreType.DMA((members // width,)),
        ],
        compiler_params=pltpu.CompilerParams(vmem_limit_bytes=VMEM_LIMIT),
        cost_estimate=COST,
        name="final",
    )(level_weight, taper, sums, *parts, *blocks)


def across(x, axis, bits):
    count = lax.axis_size(axis)
    return lax.ppermute(x, axis, [(i, i ^ bits) for i in range(count)])


def gather_line(x, bits):
    blocks = {0: x}
    for bit in bits:
        for distance in list(blocks):
            blocks[distance ^ bit] = across(blocks[distance], "rows", bit)
    return blocks


def after(x, *others):
    return lax.optimization_barrier((x, *others))[0]


def on_device(state, member_level, level_weight, obs_row, state_coords, weights):
    groups = lax.axis_size("rows")
    radius = XCOL_DEV * groups
    row_count = state.shape[0]
    observed = obs_row.shape[0]
    bits = [1 << n for n in range(groups.bit_length() - 2, 0, -1)]
    mean = -(-observed // groups)
    slots = min(observed, 4 * math.ceil((mean + 3 * math.sqrt(mean)) / 4))
    if slots % SUB * (state.shape[1] // 128) % SUB:
        slots += SUB - slots % SUB

    none = jnp.zeros((1,), jnp.int32)
    own = pick(obs_row, none, state, slots)
    first_far = across(own, "rows", bits[0])
    level_row = after(member_level, own)[None, :]
    sums, high, low, own_both, place, empty, rounds = center(
        after(obs_row, own), own, weights, level_row, after(state, own)
    )
    all_sums = sums
    for n in range(lax.axis_size("mem").bit_length() - 1):
        all_sums = jnp.concatenate([all_sums, across(all_sums, "mem", 1 << n)])

    line = gather_line(after(own, sums), bits[1:])
    line |= {b ^ bits[0]: x for b, x in gather_line(first_far, bits[1:]).items()}
    forward = line | {0: own_both}
    other = {b ^ 1: across(x, "rows", 1) for b, x in forward.items()}
    blocks = line | other
    early = [b for b in blocks if b < bits[0]]
    late = [b for b in blocks if b >= bits[0]]
    weights_pair = pairs(weights, after(other[1], all_sums))

    def cross(skip, part, high, low, held, number):
        return cross_part(level_weight, skip, level_row, place, high, low, part, held, all_sums, slots, number)

    def more(carry):
        return carry[0] < rounds[0]

    def another(carry):
        turn, part = carry
        skip = (turn * slots)[None]
        again = after(state, turn)
        block = pick(obs_row, skip, again, slots)
        _, high, low, *_ = center(obs_row, block, weights, level_row, again)
        parcels = [
            lax.all_gather(block[at : at + 64], "rows", axis=0) for at in range(0, block.shape[0], 64)
        ]
        every = jnp.concatenate(parcels, axis=1)
        me = lax.axis_index("rows")
        part = cross(skip, part, high, low, [every[me ^ b] for b in early + late], early + late)
        return turn + 1, part

    _, looped = lax.while_loop(more, another, (jnp.int32(1), empty))
    half = cross(none, looped, high, low, [blocks[b] for b in early], early)
    part = cross(none, half, high, low, [blocks[b] for b in late], late)
    parts = [part] + [across(part, "mem", b) for b in range(1, lax.axis_size("mem"))]

    far_pair = across(after(weights_pair, looped), "rows", bits[0])
    weights_line = gather_line(after(weights_pair, half), bits[1:])
    weights_line |= {b ^ bits[0]: x for b, x in gather_line(after(far_pair, part), bits[1:]).items()}
    taper = tapers(after(obs_row, part), state_coords, row_count, radius)
    return final(level_weight, parts, all_sums, taper, list(weights_line.values()), list(weights_line))


def solution(mesh):
    in_specs = (P("rows", "mem"), P("mem"), P(), P(), P(), P("rows", "mem"))
    out_specs = P("rows", "mem")
    return jax.shard_map(
        on_device, mesh=mesh, in_specs=in_specs, out_specs=out_specs, check_vma=False
    )
```

```python
import functools
import math

import jax
import jax.numpy as jnp
from jax import lax
from jax.experimental import pallas as pl
from jax.experimental.pallas import tpu as pltpu
from jax.sharding import PartitionSpec as P

LEVELS = 4
XCOL_DEV = 4
SUB = 8
VMEM_LIMIT = 48 * 1024 * 1024
COST = pl.CostEstimate(flops=1, bytes_accessed=1, transcendentals=0)
F32 = jnp.float32
BF16 = jnp.bfloat16
LANES_BOTH = (((1,), (1,)), ((), ()))
ROWS_BOTH = (((0,), (0,)), ((), ()))
PLAIN = (((1,), (0,)), ((), ()))


def dot(a, b, dims):
    return lax.dot_general(a, b, dims, preferred_element_type=F32)


def split(x, parts):
    pieces = []
    for _ in range(parts - 1):
        piece = x.astype(BF16)
        pieces.append(piece)
        x = x - piece.astype(F32)
    pieces.append(x.astype(BF16))
    return pieces


def packing(slots, members):
    lanes = members // 128
    full = slots - slots % SUB
    pieces = [(n * full, full, 0, n * 128) for n in range(lanes)] if full else []
    tail = slots - full
    if tail:
        pieces += [(lanes * full + n * tail, tail, full, n * 128) for n in range(lanes)]
    return pieces


def level_onehot(level_row):
    levels = lax.broadcasted_iota(jnp.int32, (SUB, level_row.shape[1]), 0)
    return (level_row == levels).astype(F32)


def by_level(level_row, columns):
    picked = jnp.where(level_row == 1, columns[1], columns[0])
    for level in range(2, LEVELS):
        picked = jnp.where(level_row == level, columns[level], picked)
    return picked


def pick_kernel(slots, obs_ref, skip_ref, state_ref, out_ref, list_ref, held_ref, row_ref, sem):
    rows, members = state_ref.shape
    row_first = lax.axis_index("rows") * rows
    skip = skip_ref[0]
    copy = pltpu.make_async_copy(state_ref, held_ref, sem)
    copy.start()

    def visit(j, rank):
        row = obs_ref[j] - row_first
        list_ref[rank] = row
        return rank + ((row >= 0) & (row < rows)).astype(jnp.int32)

    total = lax.fori_loop(0, obs_ref.shape[0], visit, 0, unroll=8)
    held = jnp.clip(total - skip, 0, slots)
    copy.wait()

    for slot in range(slots):
        row = jnp.clip(list_ref[skip + slot], 0, rows - 1)
        value = jnp.where(slot < held, held_ref[pl.ds(row, 1), :], 0.0)
        row_ref[slot : slot + 1, :] = value
    for at, tall, row, lane in packing(slots, members):
        out_ref[at : at + tall, :] = row_ref[row : row + tall, lane : lane + 128]


def pick(obs_row, skip, state, slots):
    smem = pl.BlockSpec(memory_space=pltpu.SMEM)
    return pl.pallas_call(
        functools.partial(pick_kernel, slots),
        out_shape=jax.ShapeDtypeStruct((slots * (state.shape[1] // 128), 128), F32),
        in_specs=[smem, smem, pl.BlockSpec(memory_space=pl.ANY)],
        out_specs=pl.BlockSpec(memory_space=pltpu.VMEM),
        scratch_shapes=[
            pltpu.SMEM((obs_row.shape[0] + slots + 1,), jnp.int32),
            pltpu.VMEM(state.shape, F32),
            pltpu.VMEM((-(-slots // SUB) * SUB, state.shape[1]), F32),
            pltpu.SemaphoreType.DMA(()),
        ],
        compiler_params=pltpu.CompilerParams(vmem_limit_bytes=VMEM_LIMIT),
        cost_estimate=COST,
        name="pick",
    )(obs_row, skip, state)


def place(slots, rows, obs_ref, place_ref, rounds_ref):
    observed = obs_ref.shape[1]
    owner = lax.div(obs_ref[...], jnp.int32(rows))
    owner_row = owner.astype(F32)
    owner_down = jnp.transpose(jnp.broadcast_to(owner_row, (SUB, observed)))[:, 0:1]
    j_down = lax.broadcasted_iota(jnp.int32, (observed, observed), 0)
    j_row = lax.broadcasted_iota(jnp.int32, (observed, observed), 1)
    earlier = (owner_down == owner_row) & (j_down < j_row)
    rank = jnp.sum(earlier.astype(F32), axis=0, keepdims=True).astype(jnp.int32)
    place_ref[0:1, :] = owner
    place_ref[1:2, :] = rank
    place_ref[2:SUB, :] = jnp.zeros((SUB - 2, observed), jnp.int32)
    rounds_ref[0] = lax.div(jnp.max(rank), jnp.int32(slots)) + 1


def center_kernel(
    slots, rows, obs_ref, own_ref, weights_ref, level_ref, state_ref, sums_ref, high_ref, low_ref,
    both_ref, place_ref, zero_ref, rounds_ref,
):
    @pl.when(pl.program_id(0) == 0)
    def _():
        held, (length, members) = own_ref.shape[0], weights_ref.shape
        both_ref[0:held, :] = own_ref[...]
        for at, tall, row, lane in packing(length, members):
            both_ref[held + at : held + at + tall, :] = weights_ref[row : row + tall, lane : lane + 128]
        place(slots, rows, obs_ref, place_ref, rounds_ref)
        zero_ref[...] = jnp.zeros_like(zero_ref)

    level_row = level_ref[...]
    onehot = level_onehot(level_row)
    counts = jnp.sum(onehot, axis=1, keepdims=True)
    state = state_ref[...]
    hot = onehot.astype(BF16)
    sums = sum(dot(hot, piece, LANES_BOTH) for piece in split(state, 3))
    sums_ref[0:LEVELS, :] = sums[0:LEVELS, :]
    sums_ref[LEVELS:SUB, :] = jnp.broadcast_to(counts[0:LEVELS, :], (LEVELS, sums.shape[1]))
    means = jnp.transpose(sums / jnp.maximum(counts, 1.0))
    columns = [means[:, level : level + 1] for level in range(LEVELS)]
    high, low = split(state - by_level(level_row, columns), 2)
    high_ref[...] = high
    low_ref[...] = low


def center(obs_row, own, weights, level_row, state):
    rows, members = state.shape
    observed = obs_row.shape[0]
    slots = own.shape[0] // (members // 128)
    tall = math.gcd(rows, 128)
    whole = lambda *shape: pl.BlockSpec(shape, lambda i: (0, 0))
    both = (own.shape[0] + weights.shape[0] * (members // 128), 128)
    return pl.pallas_call(
        functools.partial(center_kernel, slots, rows),
        out_shape=(
            jax.ShapeDtypeStruct((SUB, rows), F32),
            jax.ShapeDtypeStruct((rows, members), BF16),
            jax.ShapeDtypeStruct((rows, members), BF16),
            jax.ShapeDtypeStruct(both, F32),
            jax.ShapeDtypeStruct((SUB, observed), jnp.int32),
            jax.ShapeDtypeStruct((rows + SUB, observed), F32),
            jax.ShapeDtypeStruct((1,), jnp.int32),
        ),
        grid=(rows // tall,),
        in_specs=[
            whole(1, observed),
            whole(*own.shape),
            whole(*weights.shape),
            whole(1, members),
            pl.BlockSpec((tall, members), lambda i: (i, 0)),
        ],
        out_specs=(
            pl.BlockSpec((SUB, tall), lambda i: (0, i)),
            pl.BlockSpec((tall, members), lambda i: (i, 0)),
            pl.BlockSpec((tall, members), lambda i: (i, 0)),
            whole(*both),
            whole(SUB, observed),
            whole(rows + SUB, observed),
            pl.BlockSpec(memory_space=pltpu.SMEM),
        ),
        compiler_params=pltpu.CompilerParams(vmem_limit_bytes=VMEM_LIMIT),
        cost_estimate=COST,
        name="center",
    )(obs_row[None, :], own, weights, level_row, state)


def pair_kernel(near_ref, far_ref, pair_ref):
    length = near_ref.shape[0]
    pair_ref[0:length, :] = near_ref[...]
    members = near_ref.shape[1]
    held = far_ref.shape[0] - length * (members // 128)
    for at, tall, row, lane in packing(length, members):
        pair_ref[length + row : length + row + tall, lane : lane + 128] = far_ref[held + at : held + at + tall, :]


def pairs(near, far):
    length, members = near.shape
    vmem = pl.BlockSpec(memory_space=pltpu.VMEM)
    return pl.pallas_call(
        pair_kernel,
        out_shape=jax.ShapeDtypeStruct((2 * length, members), F32),
        in_specs=[vmem, vmem],
        out_specs=vmem,
        compiler_params=pltpu.CompilerParams(vmem_limit_bytes=VMEM_LIMIT),
        cost_estimate=COST,
        name="pairs",
    )(near, far)


def taper_kernel(radius, obs_ref, coords_ref, taper_ref):
    rows, observed = taper_ref.shape
    total = coords_ref.shape[1]
    chunk = math.gcd(total, 256)
    obs = obs_ref[...]

    def look(n, seen):
        at = pl.multiple_of(n * chunk, chunk)
        row = lax.broadcasted_iota(jnp.int32, (chunk, observed), 0) + at
        coords = coords_ref[:, pl.ds(at, chunk)].astype(F32).astype(BF16)
        return seen + dot(coords, (row == obs).astype(BF16), PLAIN)

    seen = lax.fori_loop(0, total // chunk, look, jnp.zeros((2, observed), F32), unroll=min(8, total // chunk))
    first = pl.multiple_of(lax.axis_index("rows") * rows, rows)
    own = coords_ref[:, pl.ds(first, rows)].astype(F32)
    own_x = jnp.transpose(jnp.broadcast_to(own[0:1, :], (SUB, rows)))[:, 0:1]
    own_y = jnp.transpose(jnp.broadcast_to(own[1:2, :], (SUB, rows)))[:, 0:1]
    offset_x = own_x - seen[0:1, :]
    offset_y = own_y - seen[1:2, :]
    distance = offset_x * offset_x + offset_y * offset_y
    reach = jnp.maximum(0.0, 1.0 - distance / float(radius * radius))
    taper_ref[...] = reach * reach


def tapers(obs_row, state_coords, rows, radius):
    vmem = pl.BlockSpec(memory_space=pltpu.VMEM)
    return pl.pallas_call(
        functools.partial(taper_kernel, radius),
        out_shape=jax.ShapeDtypeStruct((rows, obs_row.shape[0]), F32),
        in_specs=[vmem, vmem],
        out_specs=vmem,
        compiler_params=pltpu.CompilerParams(vmem_limit_bytes=VMEM_LIMIT),
        name="tapers",
    )(obs_row[None, :], state_coords)


def cross_kernel(number, slots, weight_ref, skip_ref, level_ref, place_ref, high_ref, low_ref, before_ref, *refs):
    blocks, (sums_ref, out_ref, o_ref, p_ref, m_ref, raw_ref) = refs[: len(number)], refs[len(number) :]
    rows = high_ref.shape[0]
    me = lax.axis_index("rows")
    skip = skip_ref[0]
    level_row = level_ref[...]
    onehot = level_onehot(level_row)
    counts = jnp.maximum(jnp.sum(onehot, axis=1, keepdims=True), 1.0)
    total = sum(
        sums_ref[at + LEVELS : at + SUB, 0:128] for at in range(0, sums_ref.shape[0], SUB)
    )
    scales = [weight_ref[level] / (total[level, 0] - 1.0) for level in range(LEVELS)]
    member_scale = by_level(level_row, scales)
    owner, rank = place_ref[0:1, :], place_ref[1:2, :]
    held = o_ref.shape[0] // 2
    padded = held // len(number)
    m_ref[...] = jnp.zeros_like(m_ref)
    for n, block_ref in enumerate(blocks):
        at = n * padded
        raw_ref[at + padded - SUB : at + padded, :] = jnp.zeros((SUB, raw_ref.shape[1]), F32)
        for start, tall, row, lane in packing(slots, raw_ref.shape[1]):
            raw_ref[at + row : at + row + tall, lane : lane + 128] = block_ref[start : start + tall, :]
        block = raw_ref[at : at + padded, :]
        columns = []
        for level in range(LEVELS):
            member = jnp.where(level_row == level, block, 0.0)
            columns.append(jnp.sum(member, axis=1, keepdims=True) / counts[level : level + 1, :])
            m_ref[at : at + padded, level : level + 1] = columns[level]
        high, low = split((block - by_level(level_row, columns)) * member_scale, 2)
        o_ref[at : at + padded, :] = high
        o_ref[held + at : held + at + padded, :] = low
        slot = lax.broadcasted_iota(jnp.int32, (padded, owner.shape[1]), 0)
        hit = (owner == (me ^ number[n])) & (rank - skip == slot) & (slot < slots)
        p_ref[at : at + padded, :] = hit.astype(BF16)
    by_piece = dot(high_ref[...], o_ref[...], LANES_BOTH)
    by_slot = by_piece[:, 0:held] + by_piece[:, held:]
    by_slot += dot(low_ref[...], o_ref[0:held, :], LANES_BOTH)
    place = p_ref[...]
    cross = sum(dot(piece, place, PLAIN) for piece in split(by_slot, 3))
    out_ref[0:rows, :] = before_ref[0:rows, :] + cross
    means = sum(dot(piece, place, ROWS_BOTH) for piece in split(m_ref[...], 3))
    out_ref[rows : rows + SUB, :] = before_ref[rows : rows + SUB, :] + means


def cross_part(level_weight, skip, level_row, place, high, low, before, blocks, sums, slots, number):
    rows, members = high.shape
    smem = pl.BlockSpec(memory_space=pltpu.SMEM)
    vmem = pl.BlockSpec(memory_space=pltpu.VMEM)
    held = len(number) * -(-slots // 16) * 16
    return pl.pallas_call(
        functools.partial(cross_kernel, number, slots),
        out_shape=jax.ShapeDtypeStruct(before.shape, F32),
        in_specs=[smem, smem] + [vmem] * (6 + len(blocks)),
        out_specs=vmem,
        scratch_shapes=[
            pltpu.VMEM((2 * held, members), BF16),
            pltpu.VMEM((held, before.shape[1]), BF16),
            pltpu.VMEM((held, SUB), F32),
            pltpu.VMEM((held, members), F32),
        ],
        compiler_params=pltpu.CompilerParams(vmem_limit_bytes=VMEM_LIMIT),
        cost_estimate=COST,
        name="cross_part",
    )(level_weight, skip, level_row, place, high, low, before, *blocks, sums)


def final_kernel(number, mem, width, weight_ref, taper_ref, sums_ref, *refs):
    parts, refs = refs[:mem], refs[mem:]
    blocks, (out_ref, w_ref, chunk, sem) = refs[: len(number)], refs[len(number) :]
    rows, observed = taper_ref.shape
    members = out_ref.shape[1]
    me = lax.axis_index("rows")

    for n, block_ref in enumerate(blocks):
        length = block_ref.shape[0] // 2
        for side in range(2):
            at = pl.multiple_of((me ^ number[n] ^ side) * length, length)
            high, low = split(block_ref[side * length : (side + 1) * length, :], 2)
            w_ref[pl.ds(at, length), :] = high
            w_ref[pl.ds(observed + at, length), :] = low
            w_ref[pl.ds(2 * observed + at, length), :] = high

    cross = sum(ref[0:rows, :] for ref in parts)
    places = range(0, mem * SUB, SUB)
    counts = [sums_ref[at + LEVELS : at + SUB, :] for at in places]
    sums = [sums_ref[at : at + LEVELS, :] for at in places]
    total = sum(counts)
    mean = sum(sums) / total
    level = lax.broadcasted_iota(jnp.int32, (LEVELS, 1), 0)
    scale = by_level(level, [weight_ref[k] for k in range(LEVELS)]) / (total - 1.0)
    seen = [ref[rows : rows + LEVELS, :] for ref in parts]
    seen_counts = [c[:, 0:1] for c in counts]
    seen_mean = sum(c * s for c, s in zip(seen_counts, seen)) / total[:, 0:1]
    left, right = [], []
    for d in range(mem):
        left.append(scale * (sums[d] - counts[d] * mean))
        right.append(jnp.where(seen_counts[d] > 0.0, seen[d] - seen_mean, 0.0))
    left = split(jnp.concatenate(left, axis=0), 2)
    right = split(jnp.concatenate(right, axis=0), 2)
    cross += dot(left[0], right[0], ROWS_BOTH)
    cross += dot(left[0], right[1], ROWS_BOTH)
    cross += dot(left[1], right[0], ROWS_BOTH)
    t_high, t_low = split(cross * taper_ref[...], 2)
    stacked = jnp.concatenate([t_high, t_high, t_low], axis=1)

    copies = []
    for n in range(members // width):
        at = n * width
        chunk[n, :, :] = dot(stacked, w_ref[:, at : at + width], PLAIN)
        copies.append(pltpu.make_async_copy(chunk.at[n], out_ref.at[:, pl.ds(at, width)], sem.at[n]))
        copies[-1].start()
    for copy in copies:
        copy.wait()


def final(level_weight, parts, sums, taper, blocks, number):
    rows, observed = taper.shape
    members = blocks[0].shape[1]
    width = math.gcd(members, 256)
    smem = pl.BlockSpec(memory_space=pltpu.SMEM)
    vmem = pl.BlockSpec(memory_space=pltpu.VMEM)
    return pl.pallas_call(
        functools.partial(final_kernel, number, len(parts), width),
        out_shape=jax.ShapeDtypeStruct((rows, members), F32),
        in_specs=[smem] + [vmem] * (2 + len(parts) + len(blocks)),
        out_specs=pl.BlockSpec(memory_space=pl.ANY),
        scratch_shapes=[
            pltpu.VMEM((3 * observed, members), BF16),
            pltpu.VMEM((members // width, rows, width), F32),
            pltpu.SemaphoreType.DMA((members // width,)),
        ],
        compiler_params=pltpu.CompilerParams(vmem_limit_bytes=VMEM_LIMIT),
        cost_estimate=COST,
        name="final",
    )(level_weight, taper, sums, *parts, *blocks)


def across(x, axis, bits):
    count = lax.axis_size(axis)
    return lax.ppermute(x, axis, [(i, i ^ bits) for i in range(count)])


def gather_line(x, bits):
    blocks = {0: x}
    for bit in bits:
        for distance in list(blocks):
            blocks[distance ^ bit] = across(blocks[distance], "rows", bit)
    return blocks


def after(x, *others):
    return lax.optimization_barrier((x, *others))[0]


def on_device(state, member_level, level_weight, obs_row, state_coords, weights):
    groups = lax.axis_size("rows")
    radius = XCOL_DEV * groups
    row_count = state.shape[0]
    observed = obs_row.shape[0]
    bits = [1 << n for n in range(groups.bit_length() - 2, 0, -1)]
    mean = -(-observed // groups)
    slots = min(observed, 4 * math.ceil((mean + 3 * math.sqrt(mean)) / 4))
    if slots % SUB * (state.shape[1] // 128) % SUB:
        slots += SUB - slots % SUB

    none = jnp.zeros((1,), jnp.int32)
    own = pick(obs_row, none, state, slots)
    first_far = across(own, "rows", bits[0])
    level_row = after(member_level, own)[None, :]
    sums, high, low, own_both, place, empty, rounds = center(
        after(obs_row, own), own, weights, level_row, after(state, own)
    )
    all_sums = sums
    for n in range(lax.axis_size("mem").bit_length() - 1):
        all_sums = jnp.concatenate([all_sums, across(all_sums, "mem", 1 << n)])

    line = gather_line(after(own, sums), bits[1:])
    line |= {b ^ bits[0]: x for b, x in gather_line(first_far, bits[1:]).items()}
    forward = line | {0: own_both}
    other = {b ^ 1: across(x, "rows", 1) for b, x in forward.items()}
    blocks = line | other
    early = [b for b in blocks if b < bits[0]]
    late = [b for b in blocks if b >= bits[0]]
    weights_pair = pairs(weights, after(other[1], all_sums))

    def cross(skip, part, high, low, held, number):
        return cross_part(level_weight, skip, level_row, place, high, low, part, held, all_sums, slots, number)

    def more(carry):
        return carry[0] < rounds[0]

    def another(carry):
        turn, part = carry
        skip = (turn * slots)[None]
        again = after(state, turn)
        block = pick(obs_row, skip, again, slots)
        _, high, low, *_ = center(obs_row, block, weights, level_row, again)
        parcels = [
            lax.all_gather(block[at : at + 64], "rows", axis=0) for at in range(0, block.shape[0], 64)
        ]
        every = jnp.concatenate(parcels, axis=1)
        me = lax.axis_index("rows")
        part = cross(skip, part, high, low, [every[me ^ b] for b in early + late], early + late)
        return turn + 1, part

    _, looped = lax.while_loop(more, another, (jnp.int32(1), empty))
    half = cross(none, looped, high, low, [blocks[b] for b in early], early)
    part = cross(none, half, high, low, [blocks[b] for b in late], late)
    parts = [part] + [across(part, "mem", b) for b in range(1, lax.axis_size("mem"))]

    far_pair = across(after(weights_pair, looped), "rows", bits[0])
    weights_line = gather_line(after(weights_pair, half), bits[1:])
    weights_line |= {b ^ bits[0]: x for b, x in gather_line(after(far_pair, part), bits[1:]).items()}
    taper = tapers(after(obs_row, part), state_coords, row_count, radius)
    return final(level_weight, parts, all_sums, taper, list(weights_line.values()), list(weights_line))


def solution(mesh):
    in_specs = (P("rows", "mem"), P("mem"), P(), P(), P(), P("rows", "mem"))
    out_specs = P("rows", "mem")
    return jax.shard_map(
        on_device, mesh=mesh, in_specs=in_specs, out_specs=out_specs, check_vma=False
    )
```

```python
import functools
import math

import jax
import jax.numpy as jnp
from jax import lax
from jax.experimental import pallas as pl
from jax.experimental.pallas import tpu as pltpu
from jax.sharding import PartitionSpec as P

LEVELS = 4
XCOL_DEV = 4
SUB = 8
VMEM_LIMIT = 48 * 1024 * 1024
COST = pl.CostEstimate(flops=1, bytes_accessed=1, transcendentals=0)
F32 = jnp.float32
BF16 = jnp.bfloat16
LANES_BOTH = (((1,), (1,)), ((), ()))
ROWS_BOTH = (((0,), (0,)), ((), ()))
PLAIN = (((1,), (0,)), ((), ()))


def dot(a, b, dims):
    return lax.dot_general(a, b, dims, preferred_element_type=F32)


def split(x, parts):
    pieces = []
    for _ in range(parts - 1):
        piece = x.astype(BF16)
        pieces.append(piece)
        x = x - piece.astype(F32)
    pieces.append(x.astype(BF16))
    return pieces


def packing(slots, members):
    lanes = members // 128
    full = slots - slots % SUB
    pieces = [(n * full, full, 0, n * 128) for n in range(lanes)] if full else []
    tail = slots - full
    if tail:
        pieces += [(lanes * full + n * tail, tail, full, n * 128) for n in range(lanes)]
    return pieces


def level_onehot(level_row):
    levels = lax.broadcasted_iota(jnp.int32, (SUB, level_row.shape[1]), 0)
    return (level_row == levels).astype(F32)


def by_level(level_row, columns):
    picked = jnp.where(level_row == 1, columns[1], columns[0])
    for level in range(2, LEVELS):
        picked = jnp.where(level_row == level, columns[level], picked)
    return picked


def pick_kernel(slots, obs_ref, skip_ref, state_ref, out_ref, list_ref, held_ref, row_ref, sem):
    rows, members = state_ref.shape
    row_first = lax.axis_index("rows") * rows
    skip = skip_ref[0]
    copy = pltpu.make_async_copy(state_ref, held_ref, sem)
    copy.start()

    def visit(j, rank):
        row = obs_ref[j] - row_first
        list_ref[rank] = row
        return rank + ((row >= 0) & (row < rows)).astype(jnp.int32)

    total = lax.fori_loop(0, obs_ref.shape[0], visit, 0, unroll=8)
    held = jnp.clip(total - skip, 0, slots)
    copy.wait()

    for slot in range(slots):
        row = jnp.clip(list_ref[skip + slot], 0, rows - 1)
        value = jnp.where(slot < held, held_ref[pl.ds(row, 1), :], 0.0)
        row_ref[slot : slot + 1, :] = value
    for at, tall, row, lane in packing(slots, members):
        out_ref[at : at + tall, :] = row_ref[row : row + tall, lane : lane + 128]


def pick(obs_row, skip, state, slots):
    smem = pl.BlockSpec(memory_space=pltpu.SMEM)
    return pl.pallas_call(
        functools.partial(pick_kernel, slots),
        out_shape=jax.ShapeDtypeStruct((slots * (state.shape[1] // 128), 128), F32),
        in_specs=[smem, smem, pl.BlockSpec(memory_space=pl.ANY)],
        out_specs=pl.BlockSpec(memory_space=pltpu.VMEM),
        scratch_shapes=[
            pltpu.SMEM((obs_row.shape[0] + slots + 1,), jnp.int32),
            pltpu.VMEM(state.shape, F32),
            pltpu.VMEM((-(-slots // SUB) * SUB, state.shape[1]), F32),
            pltpu.SemaphoreType.DMA(()),
        ],
        compiler_params=pltpu.CompilerParams(vmem_limit_bytes=VMEM_LIMIT),
        cost_estimate=COST,
        name="pick",
    )(obs_row, skip, state)


def place(slots, rows, obs_ref, place_ref, rounds_ref):
    observed = obs_ref.shape[1]
    owner = lax.div(obs_ref[...], jnp.int32(rows))
    owner_row = owner.astype(F32)
    owner_down = jnp.transpose(jnp.broadcast_to(owner_row, (SUB, observed)))[:, 0:1]
    j_down = lax.broadcasted_iota(jnp.int32, (observed, observed), 0)
    j_row = lax.broadcasted_iota(jnp.int32, (observed, observed), 1)
    earlier = (owner_down == owner_row) & (j_down < j_row)
    rank = jnp.sum(earlier.astype(F32), axis=0, keepdims=True).astype(jnp.int32)
    place_ref[0:1, :] = owner
    place_ref[1:2, :] = rank
    place_ref[2:SUB, :] = jnp.zeros((SUB - 2, observed), jnp.int32)
    rounds_ref[0] = lax.div(jnp.max(rank), jnp.int32(slots)) + 1


def center_kernel(
    slots, rows, obs_ref, own_ref, weights_ref, level_ref, state_ref, sums_ref, high_ref, low_ref,
    both_ref, place_ref, zero_ref, rounds_ref,
):
    @pl.when(pl.program_id(0) == 0)
    def _():
        held, (length, members) = own_ref.shape[0], weights_ref.shape
        both_ref[0:held, :] = own_ref[...]
        for at, tall, row, lane in packing(length, members):
            both_ref[held + at : held + at + tall, :] = weights_ref[row : row + tall, lane : lane + 128]
        place(slots, rows, obs_ref, place_ref, rounds_ref)
        zero_ref[...] = jnp.zeros_like(zero_ref)

    level_row = level_ref[...]
    onehot = level_onehot(level_row)
    counts = jnp.sum(onehot, axis=1, keepdims=True)
    state = state_ref[...]
    hot = onehot.astype(BF16)
    sums = sum(dot(hot, piece, LANES_BOTH) for piece in split(state, 3))
    sums_ref[0:LEVELS, :] = sums[0:LEVELS, :]
    sums_ref[LEVELS:SUB, :] = jnp.broadcast_to(counts[0:LEVELS, :], (LEVELS, sums.shape[1]))
    means = jnp.transpose(sums / jnp.maximum(counts, 1.0))
    columns = [means[:, level : level + 1] for level in range(LEVELS)]
    high, low = split(state - by_level(level_row, columns), 2)
    high_ref[...] = high
    low_ref[...] = low


def center(obs_row, own, weights, level_row, state):
    rows, members = state.shape
    observed = obs_row.shape[0]
    slots = own.shape[0] // (members // 128)
    tall = math.gcd(rows, 128)
    whole = lambda *shape: pl.BlockSpec(shape, lambda i: (0, 0))
    both = (own.shape[0] + weights.shape[0] * (members // 128), 128)
    return pl.pallas_call(
        functools.partial(center_kernel, slots, rows),
        out_shape=(
            jax.ShapeDtypeStruct((SUB, rows), F32),
            jax.ShapeDtypeStruct((rows, members), BF16),
            jax.ShapeDtypeStruct((rows, members), BF16),
            jax.ShapeDtypeStruct(both, F32),
            jax.ShapeDtypeStruct((SUB, observed), jnp.int32),
            jax.ShapeDtypeStruct((rows + SUB, observed), F32),
            jax.ShapeDtypeStruct((1,), jnp.int32),
        ),
        grid=(rows // tall,),
        in_specs=[
            whole(1, observed),
            whole(*own.shape),
            whole(*weights.shape),
            whole(1, members),
            pl.BlockSpec((tall, members), lambda i: (i, 0)),
        ],
        out_specs=(
            pl.BlockSpec((SUB, tall), lambda i: (0, i)),
            pl.BlockSpec((tall, members), lambda i: (i, 0)),
            pl.BlockSpec((tall, members), lambda i: (i, 0)),
            whole(*both),
            whole(SUB, observed),
            whole(rows + SUB, observed),
            pl.BlockSpec(memory_space=pltpu.SMEM),
        ),
        compiler_params=pltpu.CompilerParams(vmem_limit_bytes=VMEM_LIMIT),
        cost_estimate=COST,
        name="center",
    )(obs_row[None, :], own, weights, level_row, state)


def pair_kernel(near_ref, far_ref, pair_ref):
    length = near_ref.shape[0]
    pair_ref[0:length, :] = near_ref[...]
    members = near_ref.shape[1]
    held = far_ref.shape[0] - length * (members // 128)
    for at, tall, row, lane in packing(length, members):
        pair_ref[length + row : length + row + tall, lane : lane + 128] = far_ref[held + at : held + at + tall, :]


def pairs(near, far):
    length, members = near.shape
    vmem = pl.BlockSpec(memory_space=pltpu.VMEM)
    return pl.pallas_call(
        pair_kernel,
        out_shape=jax.ShapeDtypeStruct((2 * length, members), F32),
        in_specs=[vmem, vmem],
        out_specs=vmem,
        compiler_params=pltpu.CompilerParams(vmem_limit_bytes=VMEM_LIMIT),
        cost_estimate=COST,
        name="pairs",
    )(near, far)


def taper_kernel(radius, obs_ref, coords_ref, taper_ref):
    rows, observed = taper_ref.shape
    total = coords_ref.shape[1]
    chunk = math.gcd(total, 256)
    obs = obs_ref[...]

    def look(n, seen):
        at = pl.multiple_of(n * chunk, chunk)
        row = lax.broadcasted_iota(jnp.int32, (chunk, observed), 0) + at
        coords = coords_ref[:, pl.ds(at, chunk)].astype(F32).astype(BF16)
        return seen + dot(coords, (row == obs).astype(BF16), PLAIN)

    seen = lax.fori_loop(0, total // chunk, look, jnp.zeros((2, observed), F32), unroll=min(8, total // chunk))
    first = pl.multiple_of(lax.axis_index("rows") * rows, rows)
    own = coords_ref[:, pl.ds(first, rows)].astype(F32)
    own_x = jnp.transpose(jnp.broadcast_to(own[0:1, :], (SUB, rows)))[:, 0:1]
    own_y = jnp.transpose(jnp.broadcast_to(own[1:2, :], (SUB, rows)))[:, 0:1]
    offset_x = own_x - seen[0:1, :]
    offset_y = own_y - seen[1:2, :]
    distance = offset_x * offset_x + offset_y * offset_y
    reach = jnp.maximum(0.0, 1.0 - distance / float(radius * radius))
    taper_ref[...] = reach * reach


def tapers(obs_row, state_coords, rows, radius):
    vmem = pl.BlockSpec(memory_space=pltpu.VMEM)
    return pl.pallas_call(
        functools.partial(taper_kernel, radius),
        out_shape=jax.ShapeDtypeStruct((rows, obs_row.shape[0]), F32),
        in_specs=[vmem, vmem],
        out_specs=vmem,
        compiler_params=pltpu.CompilerParams(vmem_limit_bytes=VMEM_LIMIT),
        name="tapers",
    )(obs_row[None, :], state_coords)


def cross_kernel(number, slots, weight_ref, skip_ref, level_ref, place_ref, high_ref, low_ref, before_ref, *refs):
    blocks, (sums_ref, out_ref, o_ref, p_ref, m_ref, raw_ref) = refs[: len(number)], refs[len(number) :]
    rows = high_ref.shape[0]
    me = lax.axis_index("rows")
    skip = skip_ref[0]
    level_row = level_ref[...]
    onehot = level_onehot(level_row)
    counts = jnp.maximum(jnp.sum(onehot, axis=1, keepdims=True), 1.0)
    total = sum(
        sums_ref[at + LEVELS : at + SUB, 0:128] for at in range(0, sums_ref.shape[0], SUB)
    )
    scales = [weight_ref[level] / (total[level, 0] - 1.0) for level in range(LEVELS)]
    member_scale = by_level(level_row, scales)
    owner, rank = place_ref[0:1, :], place_ref[1:2, :]
    held = o_ref.shape[0] // 2
    padded = held // len(number)
    m_ref[...] = jnp.zeros_like(m_ref)
    for n, block_ref in enumerate(blocks):
        at = n * padded
        raw_ref[at + padded - SUB : at + padded, :] = jnp.zeros((SUB, raw_ref.shape[1]), F32)
        for start, tall, row, lane in packing(slots, raw_ref.shape[1]):
            raw_ref[at + row : at + row + tall, lane : lane + 128] = block_ref[start : start + tall, :]
        block = raw_ref[at : at + padded, :]
        columns = []
        for level in range(LEVELS):
            member = jnp.where(level_row == level, block, 0.0)
            columns.append(jnp.sum(member, axis=1, keepdims=True) / counts[level : level + 1, :])
            m_ref[at : at + padded, level : level + 1] = columns[level]
        high, low = split((block - by_level(level_row, columns)) * member_scale, 2)
        o_ref[at : at + padded, :] = high
        o_ref[held + at : held + at + padded, :] = low
        slot = lax.broadcasted_iota(jnp.int32, (padded, owner.shape[1]), 0)
        hit = (owner == (me ^ number[n])) & (rank - skip == slot) & (slot < slots)
        p_ref[at : at + padded, :] = hit.astype(BF16)
    by_piece = dot(high_ref[...], o_ref[...], LANES_BOTH)
    by_slot = by_piece[:, 0:held] + by_piece[:, held:]
    by_slot += dot(low_ref[...], o_ref[0:held, :], LANES_BOTH)
    place = p_ref[...]
    cross = sum(dot(piece, place, PLAIN) for piece in split(by_slot, 3))
    out_ref[0:rows, :] = before_ref[0:rows, :] + cross
    means = sum(dot(piece, place, ROWS_BOTH) for piece in split(m_ref[...], 3))
    out_ref[rows : rows + SUB, :] = before_ref[rows : rows + SUB, :] + means


def cross_part(level_weight, skip, level_row, place, high, low, before, blocks, sums, slots, number):
    rows, members = high.shape
    smem = pl.BlockSpec(memory_space=pltpu.SMEM)
    vmem = pl.BlockSpec(memory_space=pltpu.VMEM)
    held = len(number) * -(-slots // 16) * 16
    return pl.pallas_call(
        functools.partial(cross_kernel, number, slots),
        out_shape=jax.ShapeDtypeStruct(before.shape, F32),
        in_specs=[smem, smem] + [vmem] * (6 + len(blocks)),
        out_specs=vmem,
        scratch_shapes=[
            pltpu.VMEM((2 * held, members), BF16),
            pltpu.VMEM((held, before.shape[1]), BF16),
            pltpu.VMEM((held, SUB), F32),
            pltpu.VMEM((held, members), F32),
        ],
        compiler_params=pltpu.CompilerParams(vmem_limit_bytes=VMEM_LIMIT),
        cost_estimate=COST,
        name="cross_part",
    )(level_weight, skip, level_row, place, high, low, before, *blocks, sums)


def final_kernel(number, mem, width, weight_ref, taper_ref, sums_ref, *refs):
    parts, refs = refs[:mem], refs[mem:]
    blocks, (out_ref, w_ref, chunk, sem) = refs[: len(number)], refs[len(number) :]
    rows, observed = taper_ref.shape
    members = out_ref.shape[1]
    me = lax.axis_index("rows")

    for n, block_ref in enumerate(blocks):
        length = block_ref.shape[0] // 2
        for side in range(2):
            at = pl.multiple_of((me ^ number[n] ^ side) * length, length)
            high, low = split(block_ref[side * length : (side + 1) * length, :], 2)
            w_ref[pl.ds(at, length), :] = high
            w_ref[pl.ds(observed + at, length), :] = low
            w_ref[pl.ds(2 * observed + at, length), :] = high

    cross = sum(ref[0:rows, :] for ref in parts)
    places = range(0, mem * SUB, SUB)
    counts = [sums_ref[at + LEVELS : at + SUB, :] for at in places]
    sums = [sums_ref[at : at + LEVELS, :] for at in places]
    total = sum(counts)
    mean = sum(sums) / total
    level = lax.broadcasted_iota(jnp.int32, (LEVELS, 1), 0)
    scale = by_level(level, [weight_ref[k] for k in range(LEVELS)]) / (total - 1.0)
    seen = [ref[rows : rows + LEVELS, :] for ref in parts]
    seen_counts = [c[:, 0:1] for c in counts]
    seen_mean = sum(c * s for c, s in zip(seen_counts, seen)) / total[:, 0:1]
    left, right = [], []
    for d in range(mem):
        left.append(scale * (sums[d] - counts[d] * mean))
        right.append(jnp.where(seen_counts[d] > 0.0, seen[d] - seen_mean, 0.0))
    left = split(jnp.concatenate(left, axis=0), 2)
    right = split(jnp.concatenate(right, axis=0), 2)
    cross += dot(left[0], right[0], ROWS_BOTH)
    cross += dot(left[0], right[1], ROWS_BOTH)
    cross += dot(left[1], right[0], ROWS_BOTH)
    t_high, t_low = split(cross * taper_ref[...], 2)
    stacked = jnp.concatenate([t_high, t_high, t_low], axis=1)

    copies = []
    for n in range(members // width):
        at = n * width
        chunk[n, :, :] = dot(stacked, w_ref[:, at : at + width], PLAIN)
        copies.append(pltpu.make_async_copy(chunk.at[n], out_ref.at[:, pl.ds(at, width)], sem.at[n]))
        copies[-1].start()
    for copy in copies:
        copy.wait()


def final(level_weight, parts, sums, taper, blocks, number):
    rows, observed = taper.shape
    members = blocks[0].shape[1]
    width = math.gcd(members, 256)
    smem = pl.BlockSpec(memory_space=pltpu.SMEM)
    vmem = pl.BlockSpec(memory_space=pltpu.VMEM)
    return pl.pallas_call(
        functools.partial(final_kernel, number, len(parts), width),
        out_shape=jax.ShapeDtypeStruct((rows, members), F32),
        in_specs=[smem] + [vmem] * (2 + len(parts) + len(blocks)),
        out_specs=pl.BlockSpec(memory_space=pl.ANY),
        scratch_shapes=[
            pltpu.VMEM((3 * observed, members), BF16),
            pltpu.VMEM((members // width, rows, width), F32),
            pltpu.SemaphoreType.DMA((members // width,)),
        ],
        compiler_params=pltpu.CompilerParams(vmem_limit_bytes=VMEM_LIMIT),
        cost_estimate=COST,
        name="final",
    )(level_weight, taper, sums, *parts, *blocks)


def across(x, axis, bits):
    count = lax.axis_size(axis)
    return lax.ppermute(x, axis, [(i, i ^ bits) for i in range(count)])


def gather_line(x, bits):
    blocks = {0: x}
    for bit in bits:
        for distance in list(blocks):
            blocks[distance ^ bit] = across(blocks[distance], "rows", bit)
    return blocks


def after(x, *others):
    return lax.optimization_barrier((x, *others))[0]


def on_device(state, member_level, level_weight, obs_row, state_coords, weights):
    groups = lax.axis_size("rows")
    radius = XCOL_DEV * groups
    row_count = state.shape[0]
    observed = obs_row.shape[0]
    bits = [1 << n for n in range(groups.bit_length() - 2, 0, -1)]
    mean = -(-observed // groups)
    slots = min(observed, 4 * math.ceil((mean + 3 * math.sqrt(mean)) / 4))
    if slots % SUB * (state.shape[1] // 128) % SUB:
        slots += SUB - slots % SUB

    none = jnp.zeros((1,), jnp.int32)
    own = pick(obs_row, none, state, slots)
    first_far = across(own, "rows", bits[0])
    level_row = after(member_level, own)[None, :]
    sums, high, low, own_both, place, empty, rounds = center(
        after(obs_row, own), own, weights, level_row, after(state, own)
    )
    all_sums = sums
    for n in range(lax.axis_size("mem").bit_length() - 1):
        all_sums = jnp.concatenate([all_sums, across(all_sums, "mem", 1 << n)])

    line = gather_line(after(own, sums), bits[1:])
    line |= {b ^ bits[0]: x for b, x in gather_line(first_far, bits[1:]).items()}
    forward = line | {0: own_both}
    other = {b ^ 1: across(x, "rows", 1) for b, x in forward.items()}
    blocks = line | other
    early = [b for b in blocks if b % 2 == 0 or b in (1, bits[0] ^ 1)]
    late = [b for b in blocks if b not in early]
    weights_pair = pairs(weights, after(other[1], all_sums))

    def cross(skip, part, high, low, held, number):
        return cross_part(level_weight, skip, level_row, place, high, low, part, held, all_sums, slots, number)

    def more(carry):
        return carry[0] < rounds[0]

    def another(carry):
        turn, part = carry
        skip = (turn * slots)[None]
        again = after(state, turn)
        block = pick(obs_row, skip, again, slots)
        _, high, low, *_ = center(obs_row, block, weights, level_row, again)
        parcels = [
            lax.all_gather(block[at : at + 64], "rows", axis=0) for at in range(0, block.shape[0], 64)
        ]
        every = jnp.concatenate(parcels, axis=1)
        me = lax.axis_index("rows")
        part = cross(skip, part, high, low, [every[me ^ b] for b in early + late], early + late)
        return turn + 1, part

    _, looped = lax.while_loop(more, another, (jnp.int32(1), empty))
    half = cross(none, looped, high, low, [blocks[b] for b in early], early)
    part = cross(none, half, high, low, [blocks[b] for b in late], late)
    parts = [part] + [across(part, "mem", b) for b in range(1, lax.axis_size("mem"))]

    far_pair = across(after(weights_pair, looped), "rows", bits[0])
    weights_line = gather_line(after(weights_pair, half), bits[1:])
    weights_line |= {b ^ bits[0]: x for b, x in gather_line(after(far_pair, part), bits[1:]).items()}
    taper = tapers(after(obs_row, part), state_coords, row_count, radius)
    return final(level_weight, parts, all_sums, taper, list(weights_line.values()), list(weights_line))


def solution(mesh):
    in_specs = (P("rows", "mem"), P("mem"), P(), P(), P(), P("rows", "mem"))
    out_specs = P("rows", "mem")
    return jax.shard_map(
        on_device, mesh=mesh, in_specs=in_specs, out_specs=out_specs, check_vma=False
    )
```
